256 devices in a mesh: section: 4 (over x), dp: 8 (over z_hi, core), tp: 8 (over z_lo, y).
Axes of the slice: x: 4, y: 4, z: 8 (z_hi: 4, z_lo: 2; z = z_hi * 2 + z_lo), core: 2. Of those that a mesh axis runs over, the one named last changes fastest.
Arguments:
- rollout_rows: bfloat16 [1536, 4096], P(('section', 'tp'), 'dp'), may hold values from -6 to 6
- segment_ids: int32 [1536], P(('section', 'tp')), may hold values from 0 to 11, never falling along the last dimension, each value on 1 to 768 neighbouring positions
- gate_weights: bfloat16 [4, 4096, 14336], P('section', 'dp', 'tp'), may hold values from -0.09375 to 0.09375
- up_weights: bfloat16 [4, 4096, 14336], P('section', 'dp', 'tp'), may hold values from -0.09375 to 0.09375
- down_weights: bfloat16 [4, 14336, 4096], P('section', 'tp', 'dp'), may hold values from -0.046875 to 0.046875
- head_weights: bfloat16 [4, 4096], P('section', 'dp'), may hold values from -0.09375 to 0.09375
Outputs:
- advantages: float32 [1536], P(('section', 'tp'))
- returns: float32 [1536], P(('section', 'tp'))
The draws below stay inside these ranges and needn't reach their ends.
Inputs may be any that keep to these rules, and one draw needn't show every extreme that they name: `segment_ids`: ids never fall along the pack; each response holds 1 to 768 consecutive rows, one exactly 768; all 12 responses occur.
All inputs are finite; a program needn't handle non-finite values.
Results may differ from the reference program's by a relative error of at most 0.00076.
Values may be sent and summed in bfloat16 or wider, within the bound.
No kernel may reach another device: no remote copies, remote signals or barrier semaphores. Data moves between devices by JAX's collectives and lax.ppermute only.
A program may use at most 128 MiB of HBM per device.

```python
import math
import jax
import jax.numpy as jnp
import numpy as np
from jax import lax

D = 4096
FF = 14336
TOKENS = 1536
RESP = 12
LMAX = 768
N_SECTION = 4


def level_of(own_key, shape, shards, low, top_value):
    loudness, own = 1.0, jax.random.fold_in(own_key, 6)
    for position, shards_of in shards:
        draws = jnp.exp(jax.random.uniform(jax.random.fold_in(own, position), (shards_of,), jnp.float32, low / len(shards), top_value / len(shards)))
        loudness = loudness * jnp.repeat(draws, shape[position] // shards_of).reshape([-1 if axis == position else 1 for axis in range(len(shape))])
    return loudness


def length_profile(amount, total, most, slope):
    loads = [(1 << 20) // math.isqrt(rank ** slope) + 1 for rank in range(2, amount + 1)]
    rest, holding = total - most - (amount - 1), [1] * (amount - 1)
    while rest > 0:
        free = [i for i in range(amount - 1) if holding[i] < most]
        pool, left = sum([loads[i] for i in free]), rest
        for i in free:
            addition = min(most - holding[i], max(1, left * loads[i] // pool), rest)
            holding[i] = holding[i] + addition
            rest = rest - addition
    return np.array([most] + holding)


def uneven(own_key, amount, total, reach, slope):
    if amount == 2:
        one = jax.random.randint(own_key, (), max(1, total - reach), min(reach, total - 1) + 1)
        return jnp.stack([one, total - one])
    lengths = jnp.asarray(length_profile(amount, total, reach, slope), jnp.int32)
    couples = (amount - 1) // 2
    giver, receiver = lengths[1:1 + 2 * couples:2], lengths[2:2 + 2 * couples:2]
    room = jnp.minimum(giver - 1, reach - receiver)
    moved = jax.random.randint(jax.random.fold_in(own_key, 1), (couples,), 0, 1 << 20) % (room + 1)
    lengths = lengths.at[1:1 + 2 * couples:2].set(giver - moved).at[2:2 + 2 * couples:2].set(receiver + moved)
    return lengths[jax.random.permutation(jax.random.fold_in(own_key, 2), amount)]


def normal_values(own_key, extent, scale, bound, shards=(), kind=jnp.bfloat16):
    factor_of = level_of(own_key, extent, shards, -0.22, 0.18) if shards else 1.0
    drawn = jax.random.normal(own_key, extent, jnp.float32) * scale * factor_of
    return jnp.minimum(jnp.maximum(drawn, -bound), bound).astype(kind)


def setup_inputs(seed: int = 0) -> dict:
    streams_of = jax.random.split(jax.random.key(seed), 7)
    return {
        "rollout_rows": normal_values(streams_of[0], (TOKENS, D), 1.0, 6.0, ((0, 32), (1, 8))),
        "segment_ids": jnp.searchsorted(jnp.cumsum(uneven(streams_of[1], RESP, TOKENS, LMAX, 1)), jnp.arange(TOKENS), side="right").astype(jnp.int32),
        "gate_weights": normal_values(streams_of[2], (N_SECTION, D, FF), D ** -0.5, 0.09375, ((0, 4), (1, 8), (2, 8))),
        "up_weights": normal_values(streams_of[3], (N_SECTION, D, FF), D ** -0.5, 0.09375, ((0, 4), (1, 8), (2, 8))),
        "down_weights": normal_values(streams_of[4], (N_SECTION, FF, D), FF ** -0.5, 0.046875, ((0, 4), (1, 8), (2, 8))),
        "head_weights": normal_values(streams_of[5], (N_SECTION, D), D ** -0.5, 0.09375, ((0, 4), (1, 8))),
    }


epsilon = 1e-05
kl_coef = 0.2
discount = 1.0
trace_decay = 1.0

def score_model(rows, gate_matrix, up_matrix, down_matrix, head_vector):
    gate_sum = jnp.dot(rows, gate_matrix, preferred_element_type=jnp.float32)
    up_sum = jnp.dot(rows, up_matrix, preferred_element_type=jnp.float32)
    hidden = (jax.nn.silu(gate_sum) * up_sum).astype(jnp.bfloat16)
    stream = rows.astype(jnp.float32) + jnp.dot(hidden, down_matrix, preferred_element_type=jnp.float32)
    head = head_vector.astype(jnp.float32)
    squares = lax.optimization_barrier(jnp.mean(stream * stream, axis=1))
    return lax.optimization_barrier(jnp.sum(stream * head, axis=1)) / jnp.sqrt(squares + epsilon)

def reference(rollout_rows, segment_ids, gate_weights, up_weights, down_weights, head_weights):
    scores = [score_model(rollout_rows, gate_weights[m], up_weights[m], down_weights[m], head_weights[m]) for m in range(4)]
    policy_score, ref_score, reward_score, values = scores
    later_segments = jnp.concatenate((segment_ids[1:], jnp.array([-1], dtype=jnp.int32)))
    same = (later_segments == segment_ids).astype(jnp.float32)
    later_values = jnp.concatenate((values[1:], jnp.zeros((1,), jnp.float32)))
    rewards = -kl_coef * (policy_score - ref_score) + (1.0 - same) * reward_score
    deltas = rewards + discount * later_values * same - values
    factors = discount * trace_decay * same

    def advance(carried, inputs):
        delta_now, factor_now = inputs
        updated = delta_now + factor_now * carried
        return (updated, updated)
    final_state, advantages = lax.scan(advance, jnp.float32(0.0), (deltas, factors), reverse=True)
    return (advantages, advantages + values)
```

```python
import functools
import jax
import jax.numpy as jnp
from jax import lax
from jax.experimental import pallas as pl
from jax.experimental.pallas import tpu as pltpu
from jax.sharding import Mesh, PartitionSpec as P

EPSILON = 1e-05
KL_COEF = 0.2
AXES = ("section", "zhi", "core", "zlo", "y")
F32, BF16 = jnp.float32, jnp.bfloat16


def spread(block, axes):
    members = lax.axis_size(axes)
    copies = jnp.broadcast_to(block[None], (members,) + block.shape)
    return lax.all_to_all(copies, axes, split_axis=0, concat_axis=0, tiled=True)


def swap(block, axis="core"):
    return lax.ppermute(block, axis, [(0, 1), (1, 0)])


def shift(block, axis, by):
    n = lax.axis_size(axis)
    return lax.ppermute(block, axis, [(i, (i + by) % n) for i in range(n)])


NT = (((1,), (1,)), ((), ()))


def hidden_kernel(core_ref, xa_ref, xa2_ref, xb_ref, xb2_ref, gate_ref, up_ref, out_ref):
    core = core_ref[0]
    units = gate_ref.shape[2]
    rows = out_ref.shape[1]
    gate = jnp.zeros((units, rows), F32)
    up = jnp.zeros((units, rows), F32)
    for z in range(4):
        first = z < 2
        for other in range(2):
            if first:
                part = (xa2_ref if other else xa_ref)[:, 0, z]
            else:
                part = (xb2_ref if other else xb_ref)[0, :, z - 2]
            part = part.reshape(rows, part.shape[-1])
            parity = (1 - core) if other else core
            gate += lax.dot_general(gate_ref[z, parity], part, NT, preferred_element_type=F32)
            up += lax.dot_general(up_ref[z, parity], part, NT, preferred_element_type=F32)
    hidden = gate / (1.0 + jnp.exp(-gate)) * up
    out_ref[...] = hidden.astype(BF16)


def hidden_units(core, xa, xa2, xb, xb2, gate, up):
    units = gate.shape[2]
    rows = xa.shape[0] * xa.shape[3] * xa.shape[4]
    tiles = xa.shape[1]
    a_block = pl.BlockSpec((xa.shape[0], 1) + xa.shape[2:], lambda i, c: (0, i, 0, 0, 0, 0))
    b_block = pl.BlockSpec((1,) + xb.shape[1:], lambda i, c: (i, 0, 0, 0, 0, 0))
    weight = pl.BlockSpec(gate.shape, lambda i, c: (0, 0, 0, 0))
    return pl.pallas_call(
        hidden_kernel,
        grid_spec=pltpu.PrefetchScalarGridSpec(
            num_scalar_prefetch=1,
            grid=(tiles,),
            in_specs=[a_block, a_block, b_block, b_block, weight, weight],
            out_specs=pl.BlockSpec((units, rows), lambda i, c: (0, i)),
        ),
        out_shape=jax.ShapeDtypeStruct((units, rows * tiles), BF16),
        compiler_params=pltpu.CompilerParams(vmem_limit_bytes=48 << 20),
        name="hidden_units",
    )(core, xa, xa2, xb, xb2, gate, up)


def down_kernel(h_ref, down_ref, head_ref, out_ref):
    half = head_ref.shape[0] // 2
    for part in range(2):
        span = slice(part * half, (part + 1) * half)
        product = jnp.dot(down_ref[span, :], h_ref[...], preferred_element_type=F32)
        out_ref[part, 0, :half, :] = product.astype(BF16)
        along = jnp.sum(product * head_ref[span, :], axis=0, keepdims=True)
        high = along.astype(BF16).astype(F32)
        rest = along - high
        middle = rest.astype(BF16).astype(F32)
        low = rest - middle
        pad = jnp.zeros((13, along.shape[1]), F32)
        out_ref[part, 0, half:, :] = jnp.concatenate((high, middle, low, pad), axis=0).astype(BF16)


def down_product(hidden, down, head):
    units, total = hidden.shape
    tiles = 4
    rows = total // tiles
    width = down.shape[0]
    tall = width // 2 + 16
    return pl.pallas_call(
        down_kernel,
        grid=(tiles,),
        in_specs=[
            pl.BlockSpec((units, rows), lambda i: (0, i)),
            pl.BlockSpec(down.shape, lambda i: (0, 0)),
            pl.BlockSpec(head.shape, lambda i: (0, 0)),
        ],
        out_specs=pl.BlockSpec((2, 1, tall, rows), lambda i: (0, i, 0, 0)),
        out_shape=jax.ShapeDtypeStruct((2, tiles, tall, rows), BF16),
        compiler_params=pltpu.CompilerParams(vmem_limit_bytes=48 << 20),
        name="down_product",
    )(hidden, down, head)


def sums_kernel(arrived_ref, residual_ref, head_ref, out_ref):
    half = residual_ref.shape[0]
    residual = residual_ref[...].astype(F32)
    stream = residual
    along = jnp.sum(residual * head_ref[...], axis=0, keepdims=True)
    for member in range(arrived_ref.shape[0]):
        stream += arrived_ref[member, :half, :].astype(F32)
        terms = arrived_ref[member, half:, :].astype(F32)
        along += jnp.sum(terms, axis=0, keepdims=True)
    out_ref[0:1, :] = jnp.sum(stream * stream, axis=0, keepdims=True)
    out_ref[1:2, :] = along


def row_sums(arrived, residual, head):
    return pl.pallas_call(
        sums_kernel,
        out_shape=jax.ShapeDtypeStruct((2, residual.shape[1]), F32),
        name="row_sums",
    )(arrived, residual, head)


def shards(rollout_rows, segment_ids, gate_weights, up_weights, down_weights, head_weights):
    section, zhi, core, zlo, y = (lax.axis_index(axis) for axis in AXES)
    block_rows, width_part = rollout_rows.shape
    dp, tp = ("zhi", "core"), ("zlo", "y")
    owners = lax.axis_size(dp)

    gate = lax.all_to_all(gate_weights[0].T, dp, split_axis=0, concat_axis=0, tiled=True)
    up = lax.all_to_all(up_weights[0].T, dp, split_axis=0, concat_axis=0, tiled=True)
    units = gate.shape[0] // owners
    gate = gate.reshape(4, 2, units, width_part)
    up = up.reshape(4, 2, units, width_part)

    column = spread(rollout_rows, ("zhi", "zlo")).reshape(4, 2, block_rows, width_part)
    xa = spread(spread(column[:2], "y"), "section")
    xb = spread(spread(column[2:], "section"), "y")
    xa2, xb2 = swap(xa), swap(xb)
    here = core.reshape(1).astype(jnp.int32)
    hidden = hidden_units(here, xa, xa2, xb, xb2, gate, up)

    after, before = shift(hidden, "zhi", 1), shift(hidden, "zhi", -1)
    cut = units // 2
    far_top = shift(after[:cut], "zhi", 1)
    far_end = shift(before[cut:], "zhi", -1)
    far = jnp.concatenate((far_top, far_end), axis=0)
    mine = jnp.stack((hidden, after, far, before))
    theirs = swap(mine)
    both = jnp.stack((mine, theirs), axis=1)
    gathered = both.reshape(8 * units, -1)

    down = down_weights[0].reshape(4, 2, units, width_part)
    order = (zhi - jnp.arange(4)) % 4
    down = jnp.take(down, order, axis=0)
    down = jnp.where(core == 0, down, down[:, ::-1])
    down = down.reshape(8 * units, width_part).T
    head = head_weights[0].astype(F32)
    parts = down_product(gathered, down, head.reshape(width_part, 1))
    arrived = lax.all_to_all(
        parts.reshape((8,) + parts.shape[2:]), tp, split_axis=0, concat_axis=0, tiled=True
    )

    half = width_part // 2
    own_a = lax.dynamic_index_in_dim(xa, y, 1, keepdims=False)
    own_b = lax.dynamic_index_in_dim(xb, y, 0, keepdims=False)
    own = jnp.concatenate((own_a, own_b), axis=1)
    own = lax.dynamic_index_in_dim(own, zhi, 1, keepdims=False).reshape(-1, width_part)
    residual = lax.dynamic_slice_in_dim(own, zlo * half, half, 1).T
    own_head = lax.dynamic_slice_in_dim(head, zlo * half, half, 0).reshape(half, 1)
    sums = row_sums(arrived, residual, own_head)
    sums = sums + swap(sums)
    sums = sums + swap(sums, "zlo")
    sums = jnp.sum(spread(sums, "zhi"), axis=0)
    scores = sums[1] / jnp.sqrt(sums[0] / (width_part * owners) + EPSILON)

    everyone = spread(scores, ("section", "y")).reshape(4, -1)
    policy_score, ref_score, reward_score, values = everyone
    segments = spread(segment_ids, ("section", "zlo", "y"))
    flat = segments.reshape(-1)
    same_flat = jnp.concatenate((flat[1:] == flat[:-1], jnp.zeros((1,), bool)))

    def ordered(array):
        array = array.reshape(4, 2, 4, block_rows)
        return array.transpose(2, 0, 1, 3).reshape(-1)

    last = ordered(1.0 - same_flat.astype(F32))
    columns = ordered(flat)
    position = ordered(jnp.arange(flat.shape[0], dtype=jnp.int32))
    own_position = ((section * 2 + zlo) * 4 + y) * block_rows + jnp.arange(block_rows)
    reach = (segment_ids[:, None] == columns[None, :]) & (position[None, :] >= own_position[:, None])
    rewards = -KL_COEF * (policy_score - ref_score) + last * reward_score
    returns = jnp.sum(jnp.where(reach, rewards[None, :], 0.0), axis=1)
    own_values = lax.dynamic_index_in_dim(values.reshape(4, 4, 2, block_rows), y, 0, keepdims=False)
    own_values = lax.dynamic_index_in_dim(own_values, section, 0, keepdims=False)
    own_values = lax.dynamic_index_in_dim(own_values, zlo, 0, keepdims=False)
    return (returns - own_values, returns)


def solution(mesh):
    fine = Mesh(mesh.devices.reshape(4, 4, 2, 2, 4), AXES)
    dp, rows = ("zhi", "core"), ("section", "zlo", "y")
    tp = ("zlo", "y")
    return jax.shard_map(
        shards,
        mesh=fine,
        in_specs=(P(rows, dp), P(rows), P("section", dp, tp), P("section", dp, tp), P("section", tp, dp), P("section", dp)),
        out_specs=(P(rows), P(rows)),
        check_vma=False,
    )
```

```python
import functools
import jax
import jax.numpy as jnp
from jax import lax
from jax.experimental import pallas as pl
from jax.experimental.pallas import tpu as pltpu
from jax.sharding import Mesh, PartitionSpec as P

EPSILON = 1e-05
KL_COEF = 0.2
AXES = ("section", "zhi", "core", "zlo", "y")
F32, BF16 = jnp.float32, jnp.bfloat16
NT = (((1,), (1,)), ((), ()))
CHUNKS = 1
VMEM_LIMIT = 50 << 20


def spread(block, axes):
    members = lax.axis_size(axes)
    copies = jnp.broadcast_to(block[None], (members,) + block.shape)
    return lax.all_to_all(copies, axes, split_axis=0, concat_axis=0, tiled=True)


def shift(block, axis, by):
    n = lax.axis_size(axis)
    return lax.ppermute(block, axis, [(i, (i + by) % n) for i in range(n)])


def shift_flip(block, ring, pair, by, flip):
    n = lax.axis_size(ring)
    route = [(i * 2 + j, (i + by) % n * 2 + (j ^ flip)) for i in range(n) for j in range(2)]
    return lax.ppermute(block, (ring, pair), route)


def around(block, axis):
    one, three = shift(block, axis, 1), shift(block, axis, 3)
    return [block, one, shift(block, axis, 2), three]


def send_kernel(place_ref, weight_ref, *refs):
    outs, flipped, sems = refs[:8], refs[8], refs[9]
    units = outs[0].shape[0]
    tile = 256
    for t in range(weight_ref.shape[1] // tile):
        span = slice(t * tile, (t + 1) * tile)
        flipped[span, :] = weight_ref[:, span].T
    copies = []
    for r in range(8):
        by, flip = r // 2, r % 2
        target = lax.rem(place_ref[0] + by, 4) * 2 + (1 - place_ref[1] if flip else place_ref[1])
        start = pl.multiple_of(target * units, 16)
        copies.append(pltpu.make_async_copy(flipped.at[pl.ds(start, units)], outs[r], sems.at[r]))
        copies[-1].start()
    for copy in copies:
        copy.wait()


def to_send(place, weight):
    depth, total = weight.shape
    piece = jax.ShapeDtypeStruct((total // 8, depth), weight.dtype)
    return pl.pallas_call(
        send_kernel,
        in_specs=[pl.BlockSpec(memory_space=pltpu.SMEM), pl.BlockSpec(memory_space=pltpu.VMEM)],
        out_specs=[pl.BlockSpec(memory_space=pl.ANY)] * 8,
        out_shape=[piece] * 8,
        scratch_shapes=[pltpu.VMEM((total, depth), weight.dtype), pltpu.SemaphoreType.DMA((8,))],
        compiler_params=pltpu.CompilerParams(vmem_limit_bytes=VMEM_LIMIT),
        name="to_send",
    )(place, weight)


def travel(pieces):
    return [pieces[0]] + [shift_flip(pieces[r], "zhi", "core", r // 2, r % 2) for r in range(1, 8)]


def hidden_kernel(y_ref, *refs):
    a_refs, b_refs = refs[0:8], refs[8:16]
    gate_refs, up_refs = refs[16:24], refs[24:32]
    outs = refs[32 : 32 + CHUNKS]
    rows_buf, gate_buf, up_buf, row_sems, weight_sem = refs[32 + CHUNKS :]
    units = gate_buf.shape[1]
    rows = rows_buf.shape[3]
    part = rows // 4
    lanes = rows // CHUNKS

    def fetch(tile):
        for flip in range(2):
            for r in range(4):
                span = pl.ds(r * part, part)
                a, b = a_refs[flip * 4 + r], b_refs[flip * 4 + tile]
                low, high = pl.ds(0, 2), pl.ds(2, 2)
                pltpu.make_async_copy(a.at[tile], rows_buf.at[tile, flip, low, span], row_sems.at[tile]).start()
                pltpu.make_async_copy(b.at[r], rows_buf.at[tile, flip, high, span], row_sems.at[tile]).start()

    fetch(0)
    for r in range(8):
        pltpu.make_async_copy(gate_refs[r], gate_buf.at[r], weight_sem.at[0]).start()
        pltpu.make_async_copy(up_refs[r], up_buf.at[r], weight_sem.at[1]).start()
    for tile in range(1, 4):
        fetch(tile)
    pltpu.make_async_copy(gate_buf, gate_buf, weight_sem.at[0]).wait()
    pltpu.make_async_copy(up_buf, up_buf, weight_sem.at[1]).wait()

    def step(tile, carry):
        block = rows_buf.at[tile]
        pltpu.make_async_copy(block, block, row_sems.at[tile]).wait()
        gate = jnp.zeros((units, rows), F32)
        up = jnp.zeros((units, rows), F32)
        for z in range(4):
            for flip in range(2):
                held = rows_buf[tile, flip, z]
                gate += lax.dot_general(gate_buf[z * 2 + flip], held, NT, preferred_element_type=F32)
                up += lax.dot_general(up_buf[z * 2 + flip], held, NT, preferred_element_type=F32)
        hidden = (gate / (1.0 + jnp.exp(-gate)) * up).astype(BF16)
        at = lax.rem(y_ref[0] + 4 - tile, 4)
        for c in range(CHUNKS):
            span = pl.ds(pl.multiple_of(at * lanes, 128), lanes)
            outs[c][:, span] = hidden[:, c * lanes : (c + 1) * lanes]
        return carry

    lax.fori_loop(0, 4, step, 0)


def hidden_units(y, a, b, gate, up):
    units, depth = gate[0].shape
    rows = 4 * a[0].shape[2]
    anywhere = pl.BlockSpec(memory_space=pl.ANY)
    piece = jax.ShapeDtypeStruct((units, 4 * rows // CHUNKS), BF16)
    return pl.pallas_call(
        hidden_kernel,
        in_specs=[pl.BlockSpec(memory_space=pltpu.SMEM)] + [anywhere] * 32,
        out_specs=[pl.BlockSpec(memory_space=pltpu.VMEM)] * CHUNKS,
        out_shape=[piece] * CHUNKS,
        scratch_shapes=[
            pltpu.VMEM((4, 2, 4, rows, depth), BF16),
            pltpu.VMEM((8, units, depth), BF16),
            pltpu.VMEM((8, units, depth), BF16),
            pltpu.SemaphoreType.DMA((4,)),
            pltpu.SemaphoreType.DMA((2,)),
        ],
        compiler_params=pltpu.CompilerParams(vmem_limit_bytes=VMEM_LIMIT),
        name="hidden_units",
    )(y, *a, *b, *gate, *up)


def down_kernel(*refs):
    h_refs, (down_ref, head_ref, out_ref, buf, sem) = refs[:10], refs[10:]
    units = h_refs[0].shape[0]
    cut = units // 2
    starts = (0, 2 * units, 4 * units, 4 * units + cut, 6 * units)
    for flip in range(2):
        for k, start in enumerate(starts):
            ref = h_refs[flip * 5 + k]
            at = buf.at[pl.ds(start + flip * units, ref.shape[0])]
            pltpu.make_async_copy(ref, at, sem).start()
    pltpu.make_async_copy(buf, buf, sem).wait()
    half = head_ref.shape[0] // 2
    lanes = out_ref.shape[3]
    for quarter in range(4):
        columns = slice(quarter * lanes, (quarter + 1) * lanes)
        for part in range(2):
            span = slice(part * half, (part + 1) * half)
            product = jnp.dot(down_ref[span, :], buf[:, columns], preferred_element_type=F32)
            out_ref[part, quarter, :half, :] = product.astype(BF16)
            along = jnp.sum(product * head_ref[span, :], axis=0, keepdims=True)
            high = along.astype(BF16).astype(F32)
            rest = along - high
            middle = rest.astype(BF16).astype(F32)
            low = rest - middle
            pad = jnp.zeros((13, along.shape[1]), F32)
            out_ref[part, quarter, half:, :] = jnp.concatenate((high, middle, low, pad), axis=0).astype(BF16)


def down_product(pieces, down, head):
    total = pieces[0].shape[1]
    width, depth = down.shape
    anywhere, vmem = pl.BlockSpec(memory_space=pl.ANY), pl.BlockSpec(memory_space=pltpu.VMEM)
    return pl.pallas_call(
        down_kernel,
        in_specs=[anywhere] * 10 + [vmem, vmem],
        out_specs=vmem,
        out_shape=jax.ShapeDtypeStruct((2, 4, width // 2 + 16, total // 4), BF16),
        scratch_shapes=[pltpu.VMEM((depth, total), BF16), pltpu.SemaphoreType.DMA],
        compiler_params=pltpu.CompilerParams(vmem_limit_bytes=VMEM_LIMIT),
        name="down_product",
    )(*pieces, down, head)


def gathered(hidden):
    cut = hidden.shape[0] // 2
    after, before = shift(hidden, "zhi", 1), shift(hidden, "zhi", 3)
    far_top = shift(after[:cut], "zhi", 1)
    far_end = shift(before[cut:], "zhi", 3)
    mine = [hidden, after, far_top, far_end, before]
    return mine + [shift(piece, "core", 1) for piece in mine]


def sums_kernel(arrived_refs, residual_ref, head_ref, out_ref):
    half = residual_ref.shape[0]
    for c, arrived_ref in enumerate(arrived_refs):
        lanes = arrived_ref.shape[2]
        span = slice(c * lanes, (c + 1) * lanes)
        stream = residual_ref[:, span]
        along = jnp.sum(stream * head_ref[...], axis=0, keepdims=True)
        for member in range(arrived_ref.shape[0]):
            stream += arrived_ref[member, :half, :].astype(F32)
            terms = arrived_ref[member, half:, :].astype(F32)
            along += jnp.sum(terms, axis=0, keepdims=True)
        out_ref[0:1, span] = jnp.sum(stream * stream, axis=0, keepdims=True)
        out_ref[1:2, span] = along


def row_sums(arrived, residual, head):
    vmem = pl.BlockSpec(memory_space=pltpu.VMEM)
    return pl.pallas_call(
        sums_kernel,
        in_specs=[[vmem] * len(arrived), vmem, vmem],
        out_specs=vmem,
        out_shape=jax.ShapeDtypeStruct((2, residual.shape[1]), F32),
        name="row_sums",
    )(arrived, residual, head)


def finish_kernel(score_ref, returns_ref, advantages_ref, out_returns_ref, out_advantages_ref):
    scores = score_ref[...]
    out_returns_ref[...] = jnp.sum(returns_ref[...] * scores, axis=1, keepdims=True)
    out_advantages_ref[...] = jnp.sum(advantages_ref[...] * scores, axis=1, keepdims=True)


def finish(scores, to_returns, to_advantages):
    column = jax.ShapeDtypeStruct((to_returns.shape[0], 1), F32)
    return pl.pallas_call(finish_kernel, out_shape=[column, column], name="finish")(
        scores, to_returns, to_advantages
    )


def response_weights(segment_ids, section, zlo, y):
    block = segment_ids.shape[0]
    flat = spread(segment_ids, ("section", "zlo", "y")).reshape(-1)
    last = jnp.concatenate((flat[1:] != flat[:-1], jnp.ones((1,), bool)))
    four = jnp.arange(4, dtype=jnp.int32)
    sections = (section - four[:, None] - four[None, :]) % 4
    quarters = (y - four) % 4

    def ordered(array):
        array = array.reshape(4, 2, 4, block)
        array = jnp.take(jnp.take(array, sections, axis=0), quarters, axis=3)
        return array.transpose(0, 3, 1, 2, 4).reshape(1, -1)

    position = ordered(jnp.arange(flat.shape[0], dtype=jnp.int32))
    columns, last = ordered(flat), ordered(last.astype(F32))
    model = jnp.repeat((section - four) % 4, flat.shape[0])[None, :]
    factor = jnp.where(model == 0, -KL_COEF, jnp.where(model == 1, KL_COEF, jnp.where(model == 2, last, 0.0)))
    own = (((section * 2 + zlo) * 4 + y) * block + jnp.arange(block, dtype=jnp.int32))[:, None]
    reach = (segment_ids[:, None] == columns) & (position >= own)
    to_returns = jnp.where(reach, factor, 0.0)
    to_advantages = jnp.where((model == 3) & (position == own), -1.0, to_returns)
    return to_returns, to_advantages


def shards(rollout_rows, segment_ids, gate_weights, up_weights, down_weights, head_weights):
    section, zhi, core, zlo, y = (lax.axis_index(axis).astype(jnp.int32) for axis in AXES)
    block_rows, width_part = rollout_rows.shape
    owners = 8

    column = [[shift_flip(rollout_rows, "zhi", "zlo", by, flip) if by or flip else rollout_rows for flip in range(2)] for by in range(4)]
    place = jnp.stack((zhi, core))
    gate = travel(to_send(place, gate_weights[0]))
    up = travel(to_send(place, up_weights[0]))
    low = jnp.stack([jnp.where(zlo == 0, pair[0], pair[1]) for pair in column])
    high = jnp.stack([jnp.where(zlo == 0, pair[1], pair[0]) for pair in column])
    column = jnp.concatenate((low, high), axis=1)

    a = around(jnp.stack(around(column[:2], "y")), "section")
    b = around(jnp.stack(around(column[2:], "section")), "y")
    a_all = a + [shift(piece, "core", 1) for piece in a]
    b_all = b + [shift(piece, "core", 1) for piece in b]

    units = gate[0].shape[0]
    down = down_weights[0].reshape(4, 2, units, width_part)
    down = jnp.take(down, (zhi - jnp.arange(4)) % 4, axis=0)
    down = jnp.where(core == 0, down, down[:, ::-1])
    down = down.reshape(8 * units, width_part).T
    head = head_weights[0].astype(F32)
    half = width_part // 2
    own = jnp.concatenate([piece[0, 0] for piece in a], axis=0)
    residual = lax.dynamic_slice_in_dim(own, zlo * half, half, 1).T.astype(F32)
    own_head = lax.dynamic_slice_in_dim(head, zlo * half, half, 0).reshape(half, 1)
    to_returns, to_advantages = response_weights(segment_ids, section, zlo, y)
    head = head.reshape(width_part, 1)
    gate, down, residual, own_head, head, to_returns, to_advantages = lax.optimization_barrier(
        (gate, down, residual, own_head, head, to_returns, to_advantages)
    )

    chunks = hidden_units(y.reshape(1), a_all, b_all, gate, up)
    arrived = []
    for hidden in chunks:
        parts = down_product(gathered(hidden), down, head)
        parts = parts.reshape((8,) + parts.shape[2:])
        arrived.append(lax.all_to_all(parts, ("zlo", "y"), split_axis=0, concat_axis=0, tiled=True))
    sums = row_sums(arrived, residual, own_head)
    route = lambda by, flip: [(i * 2 + j, (i ^ by) * 2 + (j ^ flip)) for i in range(2) for j in range(2)]
    sums = sums + sum(lax.ppermute(sums, ("core", "zlo"), route(*way)) for way in ((1, 0), (0, 1), (1, 1)))
    one, two, three, four = around(sums, "zhi")
    sums = (one + three) + (two + four)
    scores = sums[1:] / jnp.sqrt(sums[:1] / (width_part * owners) + EPSILON)
    scores = jnp.concatenate(around(scores, "y"), axis=1)
    scores = jnp.concatenate(around(scores, "section"), axis=1)
    returns, advantages = finish(scores, to_returns, to_advantages)
    return (advantages.reshape(-1), returns.reshape(-1))


def solution(mesh):
    fine = Mesh(mesh.devices.reshape(4, 4, 2, 2, 4), AXES)
    dp, tp, rows = ("zhi", "core"), ("zlo", "y"), ("section", "zlo", "y")
    return jax.shard_map(
        shards,
        mesh=fine,
        in_specs=(
            P(rows, dp),
            P(rows),
            P("section", dp, tp),
            P("section", dp, tp),
            P("section", tp, dp),
            P("section", dp),
        ),
        out_specs=(P(rows), P(rows)),
        check_vma=False,
    )
```

```python
import jax
import jax.numpy as jnp
import numpy as np
from jax import lax
from jax.experimental import pallas as pl
from jax.experimental.pallas import tpu as pltpu
from jax.sharding import Mesh, PartitionSpec as P

EPSILON = 1e-05
KL_COEF = 0.2
AXES = ("section", "zhi", "core", "zlo", "y")
F32, BF16 = jnp.float32, jnp.bfloat16
NT = (((1,), (1,)), ((), ()))
CHUNKS = 1
VMEM_LIMIT = 50 << 20


def spread(block, axes):
    members = lax.axis_size(axes)
    copies = jnp.broadcast_to(block[None], (members,) + block.shape)
    return lax.all_to_all(copies, axes, split_axis=0, concat_axis=0, tiled=True)


def shift(block, axis, by):
    n = lax.axis_size(axis)
    return lax.ppermute(block, axis, [(i, (i + by) % n) for i in range(n)])


def around(block, axis):
    one, three = shift(block, axis, 1), shift(block, axis, 3)
    return [block, one, shift(block, axis, 2), three]


def relay(block, axis):
    one, three = shift(block, axis, 1), shift(block, axis, 3)
    cut = block.shape[0] // 2
    return [block, one, shift(one[:cut], axis, 1), shift(three[cut:], axis, 3), three]


def joined(pieces):
    own, one, far_top, far_end, three = pieces
    return jnp.stack((own, one, jnp.concatenate((far_top, far_end), axis=0), three))


def swapped(pieces):
    return [shift(piece, "core", 1) for piece in pieces]


def send_kernel(gate_ref, up_ref, out_ref):
    units = out_ref.shape[1] // 2
    tile = 256
    for first, ref in ((0, gate_ref), (units, up_ref)):
        for t in range(ref.shape[1] // tile):
            turned = ref[:, t * tile : (t + 1) * tile].T
            at = t * tile
            while at < (t + 1) * tile:
                owner, inside = at // units, at % units
                count = min((t + 1) * tile - at, units - inside)
                piece = turned[at - t * tile : at - t * tile + count, :]
                out_ref[owner, first + inside : first + inside + count, :] = piece
                at += count


def to_send(gate, up, owners):
    depth, total = gate.shape
    return pl.pallas_call(
        send_kernel,
        out_shape=jax.ShapeDtypeStruct((owners, 2 * total // owners, depth), gate.dtype),
        compiler_params=pltpu.CompilerParams(vmem_limit_bytes=VMEM_LIMIT),
        name="to_send",
    )(gate, up)


def hidden_kernel(place_ref, *refs):
    a_refs, b_refs, weight_ref = refs[0:10], refs[10:20], refs[20]
    outs = refs[21 : 21 + CHUNKS]
    rows_buf, weight_buf, row_sems, weight_sem = refs[21 + CHUNKS :]
    zhi, core, y = place_ref[0], place_ref[1], place_ref[2]
    units = weight_buf.shape[2]
    rows = rows_buf.shape[3] // 2
    part = rows // 4
    lanes = rows // CHUNKS
    low, high = pl.ds(0, 2), pl.ds(2, 2)

    def fetch(tile):
        pair, base = tile // 2, (tile % 2) * rows
        for flip in range(2):
            for r in range(4):
                span = pl.ds(base + r * part, part)
                if r == 2:
                    a = a_refs[flip * 5 + 2 + tile // 2].at[tile % 2]
                else:
                    a = a_refs[flip * 5 + (0, 1, 0, 4)[r]].at[tile]
                if tile == 2:
                    b = b_refs[flip * 5 + 2 + r // 2].at[r % 2]
                else:
                    b = b_refs[flip * 5 + (0, 1, 0, 4)[tile]].at[r]
                pltpu.make_async_copy(a, rows_buf.at[pair, flip, low, span], row_sems.at[pair]).start()
                pltpu.make_async_copy(b, rows_buf.at[pair, flip, high, span], row_sems.at[pair]).start()

    for flip in range(2):
        for z in range(4):
            parity = (1 - core) if flip else core
            owner = lax.rem(zhi + 4 - z, 4) * 2 + parity
            for half in range(2):
                source = weight_ref.at[owner, pl.ds(half * units, units)]
                pltpu.make_async_copy(source, weight_buf.at[half, z * 2 + flip], weight_sem).start()
    for tile in range(4):
        fetch(tile)
    pltpu.make_async_copy(weight_buf, weight_buf, weight_sem).wait()
    for pair in range(2):
        block = rows_buf.at[pair]
        pltpu.make_async_copy(block, block, row_sems.at[pair]).wait()
        gate = jnp.zeros((2 * rows, units), F32)
        up = jnp.zeros((2 * rows, units), F32)
        for z in range(4):
            for flip in range(2):
                held = rows_buf[pair, flip, z]
                gate += lax.dot_general(held, weight_buf[0, z * 2 + flip], NT, preferred_element_type=F32)
                up += lax.dot_general(held, weight_buf[1, z * 2 + flip], NT, preferred_element_type=F32)
        hidden = (gate / (1.0 + jnp.exp(-gate)) * up).astype(BF16).T
        for inner in range(2):
            at = lax.rem(y + 4 - (pair * 2 + inner), 4)
            for c in range(CHUNKS):
                span = pl.ds(pl.multiple_of(at * lanes, 128), lanes)
                first = inner * rows + c * lanes
                outs[c][:, span] = hidden[:, first : first + lanes]


def hidden_units(place, a, b, weights):
    owners, both, depth = weights.shape
    units = both // 2
    rows = 4 * a[0].shape[2]
    anywhere = pl.BlockSpec(memory_space=pl.ANY)
    piece = jax.ShapeDtypeStruct((units, 4 * rows // CHUNKS), BF16)
    return pl.pallas_call(
        hidden_kernel,
        in_specs=[pl.BlockSpec(memory_space=pltpu.SMEM)] + [anywhere] * 21,
        out_specs=[pl.BlockSpec(memory_space=pltpu.VMEM)] * CHUNKS,
        out_shape=[piece] * CHUNKS,
        scratch_shapes=[
            pltpu.VMEM((2, 2, 4, 2 * rows, depth), BF16),
            pltpu.VMEM((2, owners, units, depth), BF16),
            pltpu.SemaphoreType.DMA((2,)),
            pltpu.SemaphoreType.DMA,
        ],
        compiler_params=pltpu.CompilerParams(vmem_limit_bytes=VMEM_LIMIT),
        name="hidden_units",
    )(place, *a, *b, weights)


def turn_kernel(place_ref, down_ref, out_ref, buf, sems):
    zhi, core = place_ref[0], place_ref[1]
    units = buf.shape[1]
    copies = []
    for k in range(8):
        owner = lax.rem(zhi + 4 - k // 2, 4) * 2 + ((1 - core) if k % 2 else core)
        source = down_ref.at[pl.ds(pl.multiple_of(owner * units, 16), units)]
        copies.append(pltpu.make_async_copy(source, buf.at[k], sems.at[k]))
        copies[-1].start()
    for k in range(0, 8, 4):
        for copy in copies[k : k + 4]:
            copy.wait()
        block = buf[k : k + 4].reshape(4 * units, buf.shape[2])
        out_ref[:, k * units : (k + 4) * units] = block.T


def turned(place, down):
    total, width = down.shape
    return pl.pallas_call(
        turn_kernel,
        in_specs=[pl.BlockSpec(memory_space=pltpu.SMEM), pl.BlockSpec(memory_space=pl.ANY)],
        out_specs=pl.BlockSpec(memory_space=pltpu.VMEM),
        out_shape=jax.ShapeDtypeStruct((width, total), down.dtype),
        scratch_shapes=[pltpu.VMEM((8, total // 8, width), down.dtype), pltpu.SemaphoreType.DMA((8,))],
        compiler_params=pltpu.CompilerParams(vmem_limit_bytes=VMEM_LIMIT),
        name="turned",
    )(place, down)


def down_kernel(*refs):
    h_refs, (down_ref, head_ref, out_ref, buf, sem) = refs[:10], refs[10:]
    units = h_refs[0].shape[0]
    cut = units // 2
    starts = (0, 2 * units, 4 * units, 4 * units + cut, 6 * units)
    for flip in range(2):
        for k, start in enumerate(starts):
            ref = h_refs[flip * 5 + k]
            at = buf.at[pl.ds(start + flip * units, ref.shape[0])]
            pltpu.make_async_copy(ref, at, sem).start()
    pltpu.make_async_copy(buf, buf, sem).wait()
    half = head_ref.shape[0] // 2
    lanes = out_ref.shape[3]
    for quarter in range(4):
        columns = slice(quarter * lanes, (quarter + 1) * lanes)
        for part in range(2):
            span = slice(part * half, (part + 1) * half)
            product = jnp.dot(down_ref[span, :], buf[:, columns], preferred_element_type=F32)
            out_ref[part, quarter, :half, :] = product.astype(BF16)
            along = jnp.sum(product * head_ref[span, :], axis=0, keepdims=True)
            high = along.astype(BF16).astype(F32)
            rest = along - high
            middle = rest.astype(BF16).astype(F32)
            low = rest - middle
            pad = jnp.zeros((13, along.shape[1]), F32)
            out_ref[part, quarter, half:, :] = jnp.concatenate((high, middle, low, pad), axis=0).astype(BF16)


def down_product(pieces, down, head):
    total = pieces[0].shape[1]
    width, depth = down.shape
    anywhere, vmem = pl.BlockSpec(memory_space=pl.ANY), pl.BlockSpec(memory_space=pltpu.VMEM)
    return pl.pallas_call(
        down_kernel,
        in_specs=[anywhere] * 10 + [vmem, vmem],
        out_specs=vmem,
        out_shape=jax.ShapeDtypeStruct((2, 4, width // 2 + 16, total // 4), BF16),
        scratch_shapes=[pltpu.VMEM((depth, total), BF16), pltpu.SemaphoreType.DMA],
        compiler_params=pltpu.CompilerParams(vmem_limit_bytes=VMEM_LIMIT),
        name="down_product",
    )(*pieces, down, head)


def sums_kernel(arrived_refs, residual_ref, head_ref, out_ref):
    half = residual_ref.shape[0]
    for c, arrived_ref in enumerate(arrived_refs):
        lanes = arrived_ref.shape[2]
        span = slice(c * lanes, (c + 1) * lanes)
        stream = residual_ref[:, span]
        along = jnp.sum(stream * head_ref[...], axis=0, keepdims=True)
        for member in range(arrived_ref.shape[0]):
            stream += arrived_ref[member, :half, :].astype(F32)
            terms = arrived_ref[member, half:, :].astype(F32)
            along += jnp.sum(terms, axis=0, keepdims=True)
        out_ref[0:1, span] = jnp.sum(stream * stream, axis=0, keepdims=True)
        out_ref[1:2, span] = along


def row_sums(arrived, residual, head):
    vmem = pl.BlockSpec(memory_space=pltpu.VMEM)
    return pl.pallas_call(
        sums_kernel,
        in_specs=[[vmem] * len(arrived), vmem, vmem],
        out_specs=vmem,
        out_shape=jax.ShapeDtypeStruct((2, residual.shape[1]), F32),
        name="row_sums",
    )(arrived, residual, head)


def response_weights(flat, segment_ids, section, zlo, y):
    block = segment_ids.shape[0]
    last = jnp.concatenate((flat[1:] != flat[:-1], jnp.ones((1,), bool))).astype(F32)
    sections = [[(model - k) % 4 for k in range(4)] for model in range(4)]

    def ordered(array, library):
        array = array.reshape(4, 2, 4, block).transpose(2, 0, 1, 3)
        parts = [array[:, at] for around_model in sections for at in around_model]
        return library.stack(parts).reshape(4, 4, 4, 2, block).swapaxes(1, 2).reshape(1, -1)

    position = jnp.asarray(ordered(np.arange(flat.shape[0], dtype=np.int32), np))
    model = jnp.asarray(np.repeat(np.arange(4, dtype=np.int32), flat.shape[0])[None, :])
    columns, last = ordered(flat, jnp), ordered(last, jnp)
    factor = jnp.where(model == 0, -KL_COEF, jnp.where(model == 1, KL_COEF, jnp.where(model == 2, last, 0.0)))
    own = (((section * 2 + zlo) * 4 + y) * block + jnp.arange(block, dtype=jnp.int32))[:, None]
    reach = (segment_ids[:, None] == columns) & (position >= own)
    to_returns = jnp.where(reach, factor, 0.0)
    to_advantages = jnp.where((model == 3) & (position == own), -1.0, to_returns)
    return to_returns, to_advantages


def shards(rollout_rows, segment_ids, gate_weights, up_weights, down_weights, head_weights):
    section, zhi, core, zlo, y = (lax.axis_index(axis).astype(jnp.int32) for axis in AXES)
    block_rows, width_part = rollout_rows.shape
    owners = 8
    place = jnp.stack((zhi, core, y))

    other = shift(rollout_rows, "zlo", 1)
    weights = to_send(gate_weights[0], up_weights[0], owners)
    other, weights = lax.optimization_barrier((other, weights))
    pair = jnp.concatenate((jnp.where(zlo == 0, rollout_rows, other), jnp.where(zlo == 0, other, rollout_rows)))
    column = jnp.stack(around(pair, "zhi"))
    column, weights = lax.optimization_barrier((column, weights))
    weights = lax.all_to_all(weights, ("zhi", "core"), split_axis=0, concat_axis=0, tiled=True)

    a = relay(joined(relay(column[:2], "y")), "section")
    b = relay(joined(relay(column[2:], "section")), "y")
    a, b, down, head = lax.optimization_barrier((a, b, down_weights[0], head_weights[0]))

    others = (swapped(a), swapped(b))
    down = turned(place, down)
    head = head.astype(F32)
    half = width_part // 2
    own = jnp.concatenate((a[0][0, 0], a[1][0, 0], a[2][0, 0], a[4][0, 0]), axis=0)
    residual = lax.dynamic_slice_in_dim(own, zlo * half, half, 1).T.astype(F32)
    own_head = lax.dynamic_slice_in_dim(head, zlo * half, half, 0).reshape(half, 1)
    head = head.reshape(width_part, 1)
    weights, down, head, residual, own_head = lax.optimization_barrier((weights, down, head, residual, own_head))

    (hidden,) = hidden_units(place, a + others[0], b + others[1], weights)
    hidden, segment_ids = lax.optimization_barrier((hidden, segment_ids))
    flat = spread(segment_ids, ("section", "zlo", "y")).reshape(-1)

    cut = hidden.shape[0] // 2
    one, three = shift(hidden, "zhi", 1), shift(hidden, "zhi", 3)
    one, three, flat = lax.optimization_barrier((one, three, flat))
    to_returns, to_advantages = response_weights(flat, segment_ids, section, zlo, y)
    mine = [hidden, one, shift(one[:cut], "zhi", 1), shift(three[cut:], "zhi", 3), three]
    parts = down_product(mine + swapped(mine), down, head)
    parts = parts.reshape((8,) + parts.shape[2:])
    parts, to_returns, to_advantages = lax.optimization_barrier((parts, to_returns, to_advantages))
    arrived = lax.all_to_all(parts, ("zlo", "y"), split_axis=0, concat_axis=0, tiled=True)
    sums = row_sums([arrived], residual, own_head)
    sums = jnp.sum(spread(sums, ("zhi", "core", "zlo")), axis=0)
    scores = sums[1] / jnp.sqrt(sums[0] / (width_part * owners) + EPSILON)
    scores = spread(scores, ("section", "y")).reshape(1, -1)
    return (jnp.sum(to_advantages * scores, axis=1), jnp.sum(to_returns * scores, axis=1))


def solution(mesh):
    fine = Mesh(mesh.devices.reshape(4, 4, 2, 2, 4), AXES)
    dp, tp, rows = ("zhi", "core"), ("zlo", "y"), ("section", "zlo", "y")
    return jax.shard_map(
        shards,
        mesh=fine,
        in_specs=(
            P(rows, dp),
            P(rows),
            P("section", dp, tp),
            P("section", dp, tp),
            P("section", tp, dp),
            P("section", dp),
        ),
        out_specs=(P(rows), P(rows)),
        check_vma=False,
    )
```

```python
import functools
import jax
import jax.numpy as jnp
import numpy as np
from jax import lax
from jax.experimental import pallas as pl
from jax.experimental.pallas import tpu as pltpu
from jax.sharding import Mesh, PartitionSpec as P

EPSILON = 1e-05
KL_COEF = 0.2
AXES = ("section", "zhi", "core", "zlo", "y")
F32, BF16 = jnp.float32, jnp.bfloat16
NT = (((1,), (1,)), ((), ()))
VMEM_LIMIT = 50 << 20


def spread(block, axes):
    members = lax.axis_size(axes)
    copies = jnp.broadcast_to(block[None], (members,) + block.shape)
    return lax.all_to_all(copies, axes, split_axis=0, concat_axis=0, tiled=True)


def shift(block, axis, by):
    n = lax.axis_size(axis)
    return lax.ppermute(block, axis, [(i, (i + by) % n) for i in range(n)])


def around(block, axis):
    one, three = shift(block, axis, 1), shift(block, axis, 3)
    return [block, one, shift(block, axis, 2), three]


def relay(block, axis):
    one, three = shift(block, axis, 1), shift(block, axis, 3)
    cut = block.shape[0] // 2
    return [block, one, shift(one[:cut], axis, 1), shift(three[cut:], axis, 3), three]


def joined(pieces):
    own, one, far_top, far_end, three = pieces
    return jnp.stack((own, one, jnp.concatenate((far_top, far_end), axis=0), three))


def swapped(pieces):
    return [shift(piece, "core", 1) for piece in pieces]


def send_kernel(gate_ref, up_ref, out_ref):
    units = out_ref.shape[1] // 2
    tile = 256
    for first, ref in ((0, gate_ref), (units, up_ref)):
        for t in range(ref.shape[1] // tile):
            turned = ref[:, t * tile : (t + 1) * tile].T
            at = t * tile
            while at < (t + 1) * tile:
                owner, inside = at // units, at % units
                count = min((t + 1) * tile - at, units - inside)
                piece = turned[at - t * tile : at - t * tile + count, :]
                out_ref[owner, first + inside : first + inside + count, :] = piece
                at += count


def to_send(gate, up, owners):
    depth, total = gate.shape
    return pl.pallas_call(
        send_kernel,
        out_shape=jax.ShapeDtypeStruct((owners, 2 * total // owners, depth), gate.dtype),
        compiler_params=pltpu.CompilerParams(vmem_limit_bytes=VMEM_LIMIT),
        name="to_send",
    )(gate, up)


def hidden_kernel(place_ref, *refs):
    a_refs, b_refs, weight_ref, out_ref = refs[0:10], refs[10:20], refs[20], refs[21]
    rows_buf, weight_buf, row_sems, weight_sems = refs[22:]
    zhi, core, y, chunk = (place_ref[i] for i in range(4))
    units = weight_buf.shape[1]
    rows = rows_buf.shape[3] // 2
    part = rows // 4

    def fetch(slot, flip, half, tile):
        for r in range(4):
            span = pl.ds(slot * rows + r * part, part)
            if half == 0:
                piece = a_refs[flip * 5 + 2 + tile // 2].at[tile % 2] if r == 2 else a_refs[flip * 5 + (0, 1, 0, 4)[r]].at[tile]
            else:
                piece = b_refs[flip * 5 + 2 + r // 2].at[r % 2] if tile == 2 else b_refs[flip * 5 + (0, 1, 0, 4)[tile]].at[r]
            pltpu.make_async_copy(piece, rows_buf.at[flip, half, :, span], row_sems.at[flip, half]).start()

    for flip in range(2):
        for half in range(2):
            for inner in range(2):
                z = half * 2 + inner
                parity = (1 - core) if flip else core
                source = weight_ref.at[lax.rem(zhi + 4 - z, 4) * 2 + parity]
                pltpu.make_async_copy(source, weight_buf.at[flip * 4 + z], weight_sems.at[flip * 4 + z]).start()
            for slot in range(2):
                relative = lax.rem(y + 4 - (chunk * 2 + slot), 4)
                for tile in range(4):
                    pl.when(relative == tile)(functools.partial(fetch, slot, flip, half, tile))
    gate = jnp.zeros((2 * rows, units // 2), F32)
    up = jnp.zeros((2 * rows, units // 2), F32)
    for flip in range(2):
        for half in range(2):
            block = rows_buf.at[flip, half]
            pltpu.make_async_copy(block, block, row_sems.at[flip, half]).wait()
            for inner in range(2):
                k = flip * 4 + half * 2 + inner
                pltpu.make_async_copy(weight_buf.at[k], weight_buf.at[k], weight_sems.at[k]).wait()
                held = rows_buf[flip, half, inner]
                gate += lax.dot_general(held, weight_buf[k, : units // 2], NT, preferred_element_type=F32)
                up += lax.dot_general(held, weight_buf[k, units // 2 :], NT, preferred_element_type=F32)
    out_ref[...] = (gate / (1.0 + jnp.exp(-gate)) * up).astype(BF16).T


def hidden_units(place, a, b, weights):
    owners, both, depth = weights.shape
    rows = 8 * a[0].shape[2]
    anywhere = pl.BlockSpec(memory_space=pl.ANY)
    return pl.pallas_call(
        hidden_kernel,
        in_specs=[pl.BlockSpec(memory_space=pltpu.SMEM)] + [anywhere] * 21,
        out_specs=pl.BlockSpec(memory_space=pltpu.VMEM),
        out_shape=jax.ShapeDtypeStruct((both // 2, rows), BF16),
        scratch_shapes=[
            pltpu.VMEM((2, 2, 2, rows, depth), BF16),
            pltpu.VMEM((owners, both, depth), BF16),
            pltpu.SemaphoreType.DMA((2, 2)),
            pltpu.SemaphoreType.DMA((owners,)),
        ],
        compiler_params=pltpu.CompilerParams(vmem_limit_bytes=VMEM_LIMIT),
        name="hidden_units",
    )(place, *a, *b, weights)


def turn_kernel(place_ref, down_ref, out_ref, buf, sems):
    zhi, core = place_ref[0], place_ref[1]
    units = buf.shape[1]
    copies = []
    for k in range(8):
        owner = lax.rem(zhi + 4 - k // 2, 4) * 2 + ((1 - core) if k % 2 else core)
        source = down_ref.at[pl.ds(pl.multiple_of(owner * units, 16), units)]
        copies.append(pltpu.make_async_copy(source, buf.at[k], sems.at[k]))
        copies[-1].start()
    for k in range(0, 8, 4):
        for copy in copies[k : k + 4]:
            copy.wait()
        block = buf[k : k + 4].reshape(4 * units, buf.shape[2])
        out_ref[:, k * units : (k + 4) * units] = block.T


def turned(place, down):
    total, width = down.shape
    return pl.pallas_call(
        turn_kernel,
        in_specs=[pl.BlockSpec(memory_space=pltpu.SMEM), pl.BlockSpec(memory_space=pl.ANY)],
        out_specs=pl.BlockSpec(memory_space=pltpu.VMEM),
        out_shape=jax.ShapeDtypeStruct((width, total), down.dtype),
        scratch_shapes=[pltpu.VMEM((8, total // 8, width), down.dtype), pltpu.SemaphoreType.DMA((8,))],
        compiler_params=pltpu.CompilerParams(vmem_limit_bytes=VMEM_LIMIT),
        name="turned",
    )(place, down)


def down_kernel(*refs):
    h_refs, (down_ref, head_ref, out_ref, buf, sem) = refs[:10], refs[10:]
    units = h_refs[0].shape[0]
    cut = units // 2
    starts = (0, 2 * units, 4 * units, 4 * units + cut, 6 * units)
    for flip in range(2):
        for k, start in enumerate(starts):
            ref = h_refs[flip * 5 + k]
            at = buf.at[pl.ds(start + flip * units, ref.shape[0])]
            pltpu.make_async_copy(ref, at, sem).start()
    pltpu.make_async_copy(buf, buf, sem).wait()
    width = head_ref.shape[0] // 4
    lanes = out_ref.shape[3]
    for side in range(2):
        columns = slice(side * lanes, (side + 1) * lanes)
        product = jnp.dot(down_ref[...], buf[:, columns], preferred_element_type=F32)
        for part in range(4):
            span = slice(part * width, (part + 1) * width)
            out_ref[side, part, :width, :] = product[span, :].astype(BF16)
            along = jnp.sum(product[span, :] * head_ref[span, :], axis=0, keepdims=True)
            high = along.astype(BF16).astype(F32)
            rest = along - high
            middle = rest.astype(BF16).astype(F32)
            low = rest - middle
            pad = jnp.zeros((13, along.shape[1]), F32)
            out_ref[side, part, width:, :] = jnp.concatenate((high, middle, low, pad), axis=0).astype(BF16)


def down_product(pieces, down, head):
    total = pieces[0].shape[1]
    width, depth = down.shape
    anywhere, vmem = pl.BlockSpec(memory_space=pl.ANY), pl.BlockSpec(memory_space=pltpu.VMEM)
    return pl.pallas_call(
        down_kernel,
        in_specs=[anywhere] * 10 + [vmem, vmem],
        out_specs=vmem,
        out_shape=jax.ShapeDtypeStruct((2, 4, width // 4 + 16, total // 2), BF16),
        scratch_shapes=[pltpu.VMEM((depth, total), BF16), pltpu.SemaphoreType.DMA],
        compiler_params=pltpu.CompilerParams(vmem_limit_bytes=VMEM_LIMIT),
        name="down_product",
    )(*pieces, down, head)


def own_kernel(place_ref, *refs):
    a_refs, out_ref, buf, sem = refs[:5], refs[5], refs[6], refs[7]
    y, zlo = place_ref[0], place_ref[1]
    part = a_refs[0].shape[2]

    def fetch(chunk, tile):
        for r in range(4):
            piece = a_refs[2 + tile // 2].at[tile % 2, 0] if r == 2 else a_refs[(0, 1, 0, 4)[r]].at[tile, 0]
            pltpu.make_async_copy(piece, buf.at[pl.ds((chunk * 4 + r) * part, part)], sem).start()

    for chunk in range(2):
        relative = lax.rem(y + 4 - zlo - 2 * chunk + 4, 4)
        for tile in range(4):
            pl.when(relative == tile)(functools.partial(fetch, chunk, tile))
    pltpu.make_async_copy(buf, buf, sem).wait()
    quarter = out_ref.shape[0]
    lanes = pl.ds(pl.multiple_of(y * quarter, 128), quarter)
    out_ref[...] = buf[:, lanes].T.astype(F32)


def own_block(place, a):
    part, depth = a[0].shape[2:]
    anywhere = pl.BlockSpec(memory_space=pl.ANY)
    return pl.pallas_call(
        own_kernel,
        in_specs=[pl.BlockSpec(memory_space=pltpu.SMEM)] + [anywhere] * 5,
        out_specs=pl.BlockSpec(memory_space=pltpu.VMEM),
        out_shape=jax.ShapeDtypeStruct((depth // 4, 8 * part), F32),
        scratch_shapes=[pltpu.VMEM((8 * part, depth), BF16), pltpu.SemaphoreType.DMA],
        name="own_block",
    )(place, *a)


def sums_kernel(arrived_refs, residual_ref, head_ref, out_ref):
    half = residual_ref.shape[0]
    for c, arrived_ref in enumerate(arrived_refs):
        lanes = arrived_ref.shape[2]
        span = slice(c * lanes, (c + 1) * lanes)
        stream = residual_ref[:, span]
        along = jnp.sum(stream * head_ref[...], axis=0, keepdims=True)
        for member in range(arrived_ref.shape[0]):
            stream += arrived_ref[member, :half, :].astype(F32)
            terms = arrived_ref[member, half:, :].astype(F32)
            along += jnp.sum(terms, axis=0, keepdims=True)
        out_ref[0:1, span] = jnp.sum(stream * stream, axis=0, keepdims=True)
        out_ref[1:2, span] = along


def row_sums(arrived, residual, head):
    vmem = pl.BlockSpec(memory_space=pltpu.VMEM)
    return pl.pallas_call(
        sums_kernel,
        in_specs=[[vmem] * len(arrived), vmem, vmem],
        out_specs=vmem,
        out_shape=jax.ShapeDtypeStruct((2, residual.shape[1]), F32),
        name="row_sums",
    )(arrived, residual, head)


def response_weights(flat, segment_ids, section, zlo, y):
    block = segment_ids.shape[0]
    last = jnp.concatenate((flat[1:] != flat[:-1], jnp.ones((1,), bool))).astype(F32)
    sections = [[(model - k) % 4 for k in range(4)] for model in range(4)]

    def ordered(array, library):
        array = array.reshape(4, 2, 2, 2, block).transpose(0, 3, 2, 1, 4)
        parts = [array[at] for around_model in sections for at in around_model]
        return library.stack(parts).reshape(4, 4, 2, 2, 2, block).transpose(0, 2, 3, 1, 4, 5).reshape(1, -1)

    position = jnp.asarray(ordered(np.arange(flat.shape[0], dtype=np.int32), np))
    model = jnp.asarray(np.repeat(np.arange(4, dtype=np.int32), flat.shape[0])[None, :])
    columns, last = ordered(flat, jnp), ordered(last, jnp)
    factor = jnp.where(model == 0, -KL_COEF, jnp.where(model == 1, KL_COEF, jnp.where(model == 2, last, 0.0)))
    own = (((section * 2 + zlo) * 4 + y) * block + jnp.arange(block, dtype=jnp.int32))[:, None]
    reach = (segment_ids[:, None] == columns) & (position >= own)
    to_returns = jnp.where(reach, factor, 0.0)
    to_advantages = jnp.where((model == 3) & (position == own), -1.0, to_returns)
    return to_returns, to_advantages


def shards(rollout_rows, segment_ids, gate_weights, up_weights, down_weights, head_weights):
    section, zhi, core, zlo, y = (lax.axis_index(axis).astype(jnp.int32) for axis in AXES)
    block_rows, width_part = rollout_rows.shape
    owners = 8
    place = jnp.stack((zhi, core, y))

    rows = jnp.stack(around(rollout_rows, "zhi"))
    weights = to_send(gate_weights[0], up_weights[0], owners)
    rows, weights = lax.optimization_barrier((rows, weights))
    other, other_ids = shift(rows, "zlo", 1), shift(segment_ids, "zlo", 1)
    column = jnp.concatenate((jnp.where(zlo == 0, rows, other), jnp.where(zlo == 0, other, rows)), axis=1)
    column, other_ids, weights, down, head = lax.optimization_barrier(
        (column, other_ids, weights, down_weights[0], head_weights[0])
    )
    weights = lax.all_to_all(weights, ("zhi", "core"), split_axis=0, concat_axis=0, tiled=True)

    a = relay(joined(relay(column[:2], "y")), "section")
    b = relay(joined(relay(column[2:], "section")), "y")
    a, b, other_ids = lax.optimization_barrier((a, b, other_ids))

    others = (swapped(a), swapped(b))
    down = turned(place, down)
    head = head.astype(F32)
    quarter = width_part // 4
    own_head = lax.dynamic_slice_in_dim(head, y * quarter, quarter, 0).reshape(quarter, 1)
    head = head.reshape(width_part, 1)
    ids = jnp.stack((jnp.where(zlo == 0, segment_ids, other_ids), jnp.where(zlo == 0, other_ids, segment_ids)))
    ids = jnp.stack(around(jnp.stack(around(ids, "y")), "section"))
    weights, down, head, own_head, ids = lax.optimization_barrier((weights, down, head, own_head, ids))

    places = [jnp.stack((zhi, core, y, jnp.int32(chunk))) for chunk in range(2)]
    x = (a + others[0], b + others[1], weights)
    chunks = [hidden_units(places[0], *x)]
    neighbours = [(shift(chunks[0], "zhi", 1), shift(chunks[0], "zhi", 3))]
    neighbours[0], places[1] = lax.optimization_barrier((neighbours[0], places[1]))
    chunks.append(hidden_units(places[1], *x))
    neighbours.append((shift(chunks[1], "zhi", 1), shift(chunks[1], "zhi", 3)))

    own_place, chunks[0] = lax.optimization_barrier((jnp.stack((y, zlo)), chunks[0]))
    residual = own_block(own_place, a)
    chunks[1], ids = lax.optimization_barrier((chunks[1], ids))
    four = jnp.arange(4, dtype=jnp.int32)
    ids = jnp.take(jnp.take(ids, (section - four) % 4, axis=0), (y - four) % 4, axis=1)
    flat = ids.transpose(0, 2, 1, 3).reshape(-1)
    to_returns, to_advantages = response_weights(flat, segment_ids, section, zlo, y)

    cut = chunks[0].shape[0] // 2
    pieces = []
    for hidden, (one, three) in zip(chunks, neighbours):
        pieces.append([hidden, one, shift(one[:cut], "zhi", 1), shift(three[cut:], "zhi", 3), three])
    arrived = []
    for mine in pieces:
        parts = down_product(mine + swapped(mine), down, head)
        parts = parts.reshape((8,) + parts.shape[2:])
        if arrived:
            parts, to_returns, to_advantages = lax.optimization_barrier((parts, to_returns, to_advantages))
        arrived.append(lax.all_to_all(parts, ("zlo", "y"), split_axis=0, concat_axis=0, tiled=True))
    sums = row_sums(arrived, residual, own_head)
    sums = jnp.sum(spread(sums, ("zhi", "core", "y")), axis=0)
    scores = sums[1] / jnp.sqrt(sums[0] / (width_part * owners) + EPSILON)
    scores = spread(scores, ("section", "zlo")).reshape(1, -1)
    return (jnp.sum(to_advantages * scores, axis=1), jnp.sum(to_returns * scores, axis=1))


def solution(mesh):
    fine = Mesh(mesh.devices.reshape(4, 4, 2, 2, 4), AXES)
    dp, tp, rows = ("zhi", "core"), ("zlo", "y"), ("section", "zlo", "y")
    return jax.shard_map(
        shards,
        mesh=fine,
        in_specs=(
            P(rows, dp),
            P(rows),
            P("section", dp, tp),
            P("section", dp, tp),
            P("section", tp, dp),
            P("section", dp),
        ),
        out_specs=(P(rows), P(rows)),
        check_vma=False,
    )
```

```python
import functools
import jax
import jax.numpy as jnp
import numpy as np
from jax import lax
from jax.experimental import pallas as pl
from jax.experimental.pallas import tpu as pltpu
from jax.sharding import Mesh, PartitionSpec as P

EPSILON = 1e-05
KL_COEF = 0.2
AXES = ("section", "zhi", "core", "zlo", "y")
F32, BF16 = jnp.float32, jnp.bfloat16
NT = (((1,), (1,)), ((), ()))
VMEM_LIMIT = 50 << 20


def spread(block, axes):
    members = lax.axis_size(axes)
    copies = jnp.broadcast_to(block[None], (members,) + block.shape)
    return lax.all_to_all(copies, axes, split_axis=0, concat_axis=0, tiled=True)


def shift(block, axis, by):
    n = lax.axis_size(axis)
    return lax.ppermute(block, axis, [(i, (i + by) % n) for i in range(n)])


def around(block, axis):
    one, three = shift(block, axis, 1), shift(block, axis, 3)
    return [block, one, shift(block, axis, 2), three]


def relay(block, axis):
    one, three = shift(block, axis, 1), shift(block, axis, 3)
    cut = block.shape[0] // 2
    return [block, one, shift(one[:cut], axis, 1), shift(three[cut:], axis, 3), three]


def joined(pieces):
    own, one, far_top, far_end, three = pieces
    return jnp.stack((own, one, jnp.concatenate((far_top, far_end), axis=0), three))


def swapped(pieces):
    return [shift(piece, "core", 1) for piece in pieces]


def send_kernel(gate_ref, up_ref, out_ref):
    units = out_ref.shape[1] // 2
    tile = 256
    for first, ref in ((0, gate_ref), (units, up_ref)):
        for t in range(ref.shape[1] // tile):
            turned = ref[:, t * tile : (t + 1) * tile].T
            at = t * tile
            while at < (t + 1) * tile:
                owner, inside = at // units, at % units
                count = min((t + 1) * tile - at, units - inside)
                piece = turned[at - t * tile : at - t * tile + count, :]
                out_ref[owner, first + inside : first + inside + count, :] = piece
                at += count


def to_send(gate, up, owners):
    depth, total = gate.shape
    return pl.pallas_call(
        send_kernel,
        out_shape=jax.ShapeDtypeStruct((owners, 2 * total // owners, depth), gate.dtype),
        compiler_params=pltpu.CompilerParams(vmem_limit_bytes=VMEM_LIMIT),
        name="to_send",
    )(gate, up)


def hidden_kernel(place_ref, *refs):
    a_refs, b_refs, weight_ref, out_ref = refs[0:10], refs[10:20], refs[20], refs[21]
    rows_buf, weight_buf, row_sems, weight_sems = refs[22:]
    zhi, core, y, chunk = (place_ref[i] for i in range(4))
    units = weight_buf.shape[1]
    rows = rows_buf.shape[3] // 2
    part = rows // 4

    def fetch(slot, flip, half, tile):
        for r in range(4):
            span = pl.ds(slot * rows + r * part, part)
            if half == 0:
                piece = a_refs[flip * 5 + 2 + tile // 2].at[tile % 2] if r == 2 else a_refs[flip * 5 + (0, 1, 0, 4)[r]].at[tile]
            else:
                piece = b_refs[flip * 5 + 2 + r // 2].at[r % 2] if tile == 2 else b_refs[flip * 5 + (0, 1, 0, 4)[tile]].at[r]
            pltpu.make_async_copy(piece, rows_buf.at[flip, half, :, span], row_sems.at[flip, half]).start()

    for flip in range(2):
        for half in range(2):
            for inner in range(2):
                z = half * 2 + inner
                parity = (1 - core) if flip else core
                source = weight_ref.at[lax.rem(zhi + 4 - z, 4) * 2 + parity]
                pltpu.make_async_copy(source, weight_buf.at[flip * 4 + z], weight_sems.at[flip * 4 + z]).start()
            for slot in range(2):
                relative = lax.rem(y + 4 - (chunk * 2 + slot), 4)
                for tile in range(4):
                    pl.when(relative == tile)(functools.partial(fetch, slot, flip, half, tile))
    gate = jnp.zeros((2 * rows, units // 2), F32)
    up = jnp.zeros((2 * rows, units // 2), F32)
    for flip in range(2):
        for half in range(2):
            block = rows_buf.at[flip, half]
            pltpu.make_async_copy(block, block, row_sems.at[flip, half]).wait()
            for inner in range(2):
                k = flip * 4 + half * 2 + inner
                pltpu.make_async_copy(weight_buf.at[k], weight_buf.at[k], weight_sems.at[k]).wait()
                held = rows_buf[flip, half, inner]
                gate += lax.dot_general(held, weight_buf[k, : units // 2], NT, preferred_element_type=F32)
                up += lax.dot_general(held, weight_buf[k, units // 2 :], NT, preferred_element_type=F32)
    out_ref[...] = (gate / (1.0 + jnp.exp(-gate)) * up).astype(BF16).T


def hidden_units(place, a, b, weights):
    owners, both, depth = weights.shape
    rows = 8 * a[0].shape[2]
    anywhere = pl.BlockSpec(memory_space=pl.ANY)
    return pl.pallas_call(
        hidden_kernel,
        in_specs=[pl.BlockSpec(memory_space=pltpu.SMEM)] + [anywhere] * 21,
        out_specs=pl.BlockSpec(memory_space=pltpu.VMEM),
        out_shape=jax.ShapeDtypeStruct((both // 2, rows), BF16),
        scratch_shapes=[
            pltpu.VMEM((2, 2, 2, rows, depth), BF16),
            pltpu.VMEM((owners, both, depth), BF16),
            pltpu.SemaphoreType.DMA((2, 2)),
            pltpu.SemaphoreType.DMA((owners,)),
        ],
        compiler_params=pltpu.CompilerParams(vmem_limit_bytes=VMEM_LIMIT),
        name="hidden_units",
    )(place, *a, *b, weights)


def turn_kernel(place_ref, down_ref, out_ref, buf, sems):
    zhi, core = place_ref[0], place_ref[1]
    units = buf.shape[1]
    copies = []
    for k in range(8):
        owner = lax.rem(zhi + 4 - k // 2, 4) * 2 + ((1 - core) if k % 2 else core)
        source = down_ref.at[pl.ds(pl.multiple_of(owner * units, 16), units)]
        copies.append(pltpu.make_async_copy(source, buf.at[k], sems.at[k]))
        copies[-1].start()
    for k in range(0, 8, 4):
        for copy in copies[k : k + 4]:
            copy.wait()
        block = buf[k : k + 4].reshape(4 * units, buf.shape[2])
        out_ref[:, k * units : (k + 4) * units] = block.T


def turned(place, down):
    total, width = down.shape
    return pl.pallas_call(
        turn_kernel,
        in_specs=[pl.BlockSpec(memory_space=pltpu.SMEM), pl.BlockSpec(memory_space=pl.ANY)],
        out_specs=pl.BlockSpec(memory_space=pltpu.VMEM),
        out_shape=jax.ShapeDtypeStruct((width, total), down.dtype),
        scratch_shapes=[pltpu.VMEM((8, total // 8, width), down.dtype), pltpu.SemaphoreType.DMA((8,))],
        compiler_params=pltpu.CompilerParams(vmem_limit_bytes=VMEM_LIMIT),
        name="turned",
    )(place, down)


def down_kernel(*refs):
    h_refs, (down_ref, head_ref, out_ref, buf, sem) = refs[:10], refs[10:]
    units = h_refs[0].shape[0]
    cut = units // 2
    starts = (0, 2 * units, 4 * units, 4 * units + cut, 6 * units)
    for flip in range(2):
        for k, start in enumerate(starts):
            ref = h_refs[flip * 5 + k]
            at = buf.at[pl.ds(start + flip * units, ref.shape[0])]
            pltpu.make_async_copy(ref, at, sem).start()
    pltpu.make_async_copy(buf, buf, sem).wait()
    width = head_ref.shape[0] // 4
    lanes = out_ref.shape[3]
    for side in range(2):
        columns = slice(side * lanes, (side + 1) * lanes)
        product = jnp.dot(down_ref[...], buf[:, columns], preferred_element_type=F32)
        for part in range(4):
            span = slice(part * width, (part + 1) * width)
            out_ref[side, part, :width, :] = product[span, :].astype(BF16)
            along = jnp.sum(product[span, :] * head_ref[span, :], axis=0, keepdims=True)
            high = along.astype(BF16).astype(F32)
            rest = along - high
            middle = rest.astype(BF16).astype(F32)
            low = rest - middle
            pad = jnp.zeros((13, along.shape[1]), F32)
            out_ref[side, part, width:, :] = jnp.concatenate((high, middle, low, pad), axis=0).astype(BF16)


def down_product(pieces, down, head):
    total = pieces[0].shape[1]
    width, depth = down.shape
    anywhere, vmem = pl.BlockSpec(memory_space=pl.ANY), pl.BlockSpec(memory_space=pltpu.VMEM)
    return pl.pallas_call(
        down_kernel,
        in_specs=[anywhere] * 10 + [vmem, vmem],
        out_specs=vmem,
        out_shape=jax.ShapeDtypeStruct((2, 4, width // 4 + 16, total // 2), BF16),
        scratch_shapes=[pltpu.VMEM((depth, total), BF16), pltpu.SemaphoreType.DMA],
        compiler_params=pltpu.CompilerParams(vmem_limit_bytes=VMEM_LIMIT),
        name="down_product",
    )(*pieces, down, head)


def own_kernel(place_ref, *refs):
    a_refs, out_ref, buf, sem = refs[:5], refs[5], refs[6], refs[7]
    y, zlo = place_ref[0], place_ref[1]
    part = a_refs[0].shape[2]

    def fetch(chunk, tile):
        for r in range(4):
            piece = a_refs[2 + tile // 2].at[tile % 2, 0] if r == 2 else a_refs[(0, 1, 0, 4)[r]].at[tile, 0]
            pltpu.make_async_copy(piece, buf.at[pl.ds((chunk * 4 + r) * part, part)], sem).start()

    for chunk in range(2):
        relative = lax.rem(y + 4 - zlo - 2 * chunk + 4, 4)
        for tile in range(4):
            pl.when(relative == tile)(functools.partial(fetch, chunk, tile))
    pltpu.make_async_copy(buf, buf, sem).wait()
    quarter = out_ref.shape[0]
    lanes = pl.ds(pl.multiple_of(y * quarter, 128), quarter)
    out_ref[...] = buf[:, lanes].T.astype(F32)


def own_block(place, a):
    part, depth = a[0].shape[2:]
    anywhere = pl.BlockSpec(memory_space=pl.ANY)
    return pl.pallas_call(
        own_kernel,
        in_specs=[pl.BlockSpec(memory_space=pltpu.SMEM)] + [anywhere] * 5,
        out_specs=pl.BlockSpec(memory_space=pltpu.VMEM),
        out_shape=jax.ShapeDtypeStruct((depth // 4, 8 * part), F32),
        scratch_shapes=[pltpu.VMEM((8 * part, depth), BF16), pltpu.SemaphoreType.DMA],
        name="own_block",
    )(place, *a)


def sums_kernel(arrived_refs, residual_ref, head_ref, out_ref):
    half = residual_ref.shape[0]
    for c, arrived_ref in enumerate(arrived_refs):
        lanes = arrived_ref.shape[2]
        span = slice(c * lanes, (c + 1) * lanes)
        stream = residual_ref[:, span]
        along = jnp.sum(stream * head_ref[...], axis=0, keepdims=True)
        for member in range(arrived_ref.shape[0]):
            stream += arrived_ref[member, :half, :].astype(F32)
            terms = arrived_ref[member, half:, :].astype(F32)
            along += jnp.sum(terms, axis=0, keepdims=True)
        out_ref[0:1, span] = jnp.sum(stream * stream, axis=0, keepdims=True)
        out_ref[1:2, span] = along


def row_sums(arrived, residual, head):
    vmem = pl.BlockSpec(memory_space=pltpu.VMEM)
    return pl.pallas_call(
        sums_kernel,
        in_specs=[[vmem] * len(arrived), vmem, vmem],
        out_specs=vmem,
        out_shape=jax.ShapeDtypeStruct((2, residual.shape[1]), F32),
        name="row_sums",
    )(arrived, residual, head)


def response_weights(flat, segment_ids, section, zlo, y):
    block = segment_ids.shape[0]
    last = jnp.concatenate((flat[1:] != flat[:-1], jnp.ones((1,), bool))).astype(F32)
    sections = [[(model - k) % 4 for k in range(4)] for model in range(4)]

    def ordered(array, library):
        array = array.reshape(4, 2, 2, 2, block).transpose(0, 3, 2, 1, 4)
        parts = [array[at] for around_model in sections for at in around_model]
        return library.stack(parts).reshape(4, 4, 2, 2, 2, block).transpose(0, 2, 3, 1, 4, 5).reshape(1, -1)

    position = jnp.asarray(ordered(np.arange(flat.shape[0], dtype=np.int32), np))
    model = jnp.asarray(np.repeat(np.arange(4, dtype=np.int32), flat.shape[0])[None, :])
    columns, last = ordered(flat, jnp), ordered(last, jnp)
    factor = jnp.where(model == 0, -KL_COEF, jnp.where(model == 1, KL_COEF, jnp.where(model == 2, last, 0.0)))
    own = (((section * 2 + zlo) * 4 + y) * block + jnp.arange(block, dtype=jnp.int32))[:, None]
    reach = (segment_ids[:, None] == columns) & (position >= own)
    to_returns = jnp.where(reach, factor, 0.0)
    to_advantages = jnp.where((model == 3) & (position == own), -1.0, to_returns)
    return to_returns, to_advantages


def shards(rollout_rows, segment_ids, gate_weights, up_weights, down_weights, head_weights):
    section, zhi, core, zlo, y = (lax.axis_index(axis).astype(jnp.int32) for axis in AXES)
    block_rows, width_part = rollout_rows.shape
    owners = 8
    place = jnp.stack((zhi, core, y))

    rows = jnp.stack(around(rollout_rows, "zhi"))
    weights = to_send(gate_weights[0], up_weights[0], owners)
    rows, weights = lax.optimization_barrier((rows, weights))
    other, other_ids = shift(rows, "zlo", 1), shift(segment_ids, "zlo", 1)
    column = jnp.concatenate((jnp.where(zlo == 0, rows, other), jnp.where(zlo == 0, other, rows)), axis=1)
    column, other_ids, weights, down, head = lax.optimization_barrier(
        (column, other_ids, weights, down_weights[0], head_weights[0])
    )
    weights = lax.all_to_all(weights, ("zhi", "core"), split_axis=0, concat_axis=0, tiled=True)

    a = relay(joined(relay(column[:2], "y")), "section")
    b = relay(joined(relay(column[2:], "section")), "y")
    a, b, other_ids = lax.optimization_barrier((a, b, other_ids))

    others = (swapped(a), swapped(b))
    down = turned(place, down)
    head = head.astype(F32)
    quarter = width_part // 4
    own_head = lax.dynamic_slice_in_dim(head, y * quarter, quarter, 0).reshape(quarter, 1)
    head = head.reshape(width_part, 1)
    ids = jnp.stack((jnp.where(zlo == 0, segment_ids, other_ids), jnp.where(zlo == 0, other_ids, segment_ids)))
    ids = jnp.stack(around(jnp.stack(around(ids, "y")), "section"))
    weights, down, head, own_head, ids = lax.optimization_barrier((weights, down, head, own_head, ids))

    places = [jnp.stack((zhi, core, y, jnp.int32(chunk))) for chunk in range(2)]
    x = (a + others[0], b + others[1], weights)
    first = hidden_units(places[0], *x)
    mine = relay(first, "zhi")
    theirs = [shift(first, "core", 1)]
    places[1], theirs[0] = lax.optimization_barrier((places[1], theirs[0]))
    second = hidden_units(places[1], *x)

    own_place, first = lax.optimization_barrier((jnp.stack((y, zlo)), first))
    residual = own_block(own_place, a)
    second, ids = lax.optimization_barrier((second, ids))
    four = jnp.arange(4, dtype=jnp.int32)
    ids = jnp.take(jnp.take(ids, (section - four) % 4, axis=0), (y - four) % 4, axis=1)
    flat = ids.transpose(0, 2, 1, 3).reshape(-1)
    to_returns, to_advantages = response_weights(flat, segment_ids, section, zlo, y)

    cut = second.shape[0] // 2
    one, three = shift(second, "zhi", 1), shift(second, "zhi", 3)
    top, end = one[:cut], three[cut:]
    mine[2], mine[3], _, _ = lax.optimization_barrier((mine[2], mine[3], top, end))
    pieces = [mine + theirs + swapped(mine[1:])]
    mine = [second, one, shift(top, "zhi", 1), shift(end, "zhi", 3), three]
    pieces.append(mine + swapped(mine))
    arrived = []
    for piece in pieces:
        parts = down_product(piece, down, head)
        parts = parts.reshape((8,) + parts.shape[2:])
        if arrived:
            parts, to_returns, to_advantages = lax.optimization_barrier((parts, to_returns, to_advantages))
        arrived.append(lax.all_to_all(parts, ("zlo", "y"), split_axis=0, concat_axis=0, tiled=True))
    sums = row_sums(arrived, residual, own_head)
    sums = sums + shift(sums, "core", 1)
    sums = jnp.sum(spread(sums, ("zhi", "y")), axis=0)
    scores = sums[1] / jnp.sqrt(sums[0] / (width_part * owners) + EPSILON)
    scores = spread(scores, ("section", "zlo")).reshape(1, -1)
    return (jnp.sum(to_advantages * scores, axis=1), jnp.sum(to_returns * scores, axis=1))


def solution(mesh):
    fine = Mesh(mesh.devices.reshape(4, 4, 2, 2, 4), AXES)
    dp, tp, rows = ("zhi", "core"), ("zlo", "y"), ("section", "zlo", "y")
    return jax.shard_map(
        shards,
        mesh=fine,
        in_specs=(
            P(rows, dp),
            P(rows),
            P("section", dp, tp),
            P("section", dp, tp),
            P("section", tp, dp),
            P("section", dp),
        ),
        out_specs=(P(rows), P(rows)),
        check_vma=False,
    )
```

```python
import functools
import jax
import jax.numpy as jnp
import numpy as np
from jax import lax
from jax.experimental import pallas as pl
from jax.experimental.pallas import tpu as pltpu
from jax.sharding import Mesh, PartitionSpec as P

EPSILON = 1e-05
KL_COEF = 0.2
AXES = ("section", "zhi", "core", "zlo", "y")
F32, BF16 = jnp.float32, jnp.bfloat16
NT = (((1,), (1,)), ((), ()))
VMEM_LIMIT = 50 << 20


def spread(block, axes):
    members = lax.axis_size(axes)
    copies = jnp.broadcast_to(block[None], (members,) + block.shape)
    return lax.all_to_all(copies, axes, split_axis=0, concat_axis=0, tiled=True)


def shift(block, axis, by):
    n = lax.axis_size(axis)
    return lax.ppermute(block, axis, [(i, (i + by) % n) for i in range(n)])


def around(block, axis):
    one, three = shift(block, axis, 1), shift(block, axis, 3)
    return [block, one, shift(block, axis, 2), three]


def relay(block, axis):
    one, three = shift(block, axis, 1), shift(block, axis, 3)
    cut = block.shape[0] // 2
    return [block, one, shift(one[:cut], axis, 1), shift(three[cut:], axis, 3), three]


def total_around(block, axis):
    block = block + shift(block, axis, 2)
    return block + shift(block, axis, 1)


def joined(pieces):
    own, one, far_top, far_end, three = pieces
    return jnp.stack((own, one, jnp.concatenate((far_top, far_end), axis=0), three))


def swapped(pieces):
    return [shift(piece, "core", 1) for piece in pieces]


def send_kernel(gate_ref, up_ref, out_ref):
    units = out_ref.shape[1] // 2
    tile = 256
    for first, ref in ((0, gate_ref), (units, up_ref)):
        for t in range(ref.shape[1] // tile):
            turned = ref[:, t * tile : (t + 1) * tile].T
            at = t * tile
            while at < (t + 1) * tile:
                owner, inside = at // units, at % units
                count = min((t + 1) * tile - at, units - inside)
                piece = turned[at - t * tile : at - t * tile + count, :]
                out_ref[owner, first + inside : first + inside + count, :] = piece
                at += count


def to_send(gate, up, owners):
    depth, total = gate.shape
    return pl.pallas_call(
        send_kernel,
        out_shape=jax.ShapeDtypeStruct((owners, 2 * total // owners, depth), gate.dtype),
        compiler_params=pltpu.CompilerParams(vmem_limit_bytes=VMEM_LIMIT),
        name="to_send",
    )(gate, up)


def hidden_kernel(place_ref, *refs):
    a_refs, b_refs, weight_ref, out_ref = refs[0:10], refs[10:20], refs[20], refs[21]
    rows_buf, weight_buf, row_sems, weight_sems = refs[22:]
    zhi, core, y, chunk = (place_ref[i] for i in range(4))
    units = weight_buf.shape[1]
    rows = rows_buf.shape[3] // 2
    part = rows // 4

    def fetch(slot, flip, half, tile):
        for r in range(4):
            span = pl.ds(slot * rows + r * part, part)
            if half == 0:
                piece = a_refs[flip * 5 + 2 + tile // 2].at[tile % 2] if r == 2 else a_refs[flip * 5 + (0, 1, 0, 4)[r]].at[tile]
            else:
                piece = b_refs[flip * 5 + 2 + r // 2].at[r % 2] if tile == 2 else b_refs[flip * 5 + (0, 1, 0, 4)[tile]].at[r]
            pltpu.make_async_copy(piece, rows_buf.at[flip, half, :, span], row_sems.at[flip, half]).start()

    for flip in range(2):
        for half in range(2):
            for inner in range(2):
                z = half * 2 + inner
                parity = (1 - core) if flip else core
                source = weight_ref.at[lax.rem(zhi + 4 - z, 4) * 2 + parity]
                pltpu.make_async_copy(source, weight_buf.at[flip * 4 + z], weight_sems.at[flip * 4 + z]).start()
            for slot in range(2):
                relative = lax.rem(y + 4 - (chunk * 2 + slot), 4)
                for tile in range(4):
                    pl.when(relative == tile)(functools.partial(fetch, slot, flip, half, tile))
    gate = jnp.zeros((2 * rows, units // 2), F32)
    up = jnp.zeros((2 * rows, units // 2), F32)
    for flip in range(2):
        for half in range(2):
            block = rows_buf.at[flip, half]
            pltpu.make_async_copy(block, block, row_sems.at[flip, half]).wait()
            for inner in range(2):
                k = flip * 4 + half * 2 + inner
                pltpu.make_async_copy(weight_buf.at[k], weight_buf.at[k], weight_sems.at[k]).wait()
                held = rows_buf[flip, half, inner]
                gate += lax.dot_general(held, weight_buf[k, : units // 2], NT, preferred_element_type=F32)
                up += lax.dot_general(held, weight_buf[k, units // 2 :], NT, preferred_element_type=F32)
    out_ref[...] = (gate / (1.0 + jnp.exp(-gate)) * up).astype(BF16).T


def hidden_units(place, a, b, weights):
    owners, both, depth = weights.shape
    rows = 8 * a[0].shape[2]
    anywhere = pl.BlockSpec(memory_space=pl.ANY)
    return pl.pallas_call(
        hidden_kernel,
        in_specs=[pl.BlockSpec(memory_space=pltpu.SMEM)] + [anywhere] * 21,
        out_specs=pl.BlockSpec(memory_space=pltpu.VMEM),
        out_shape=jax.ShapeDtypeStruct((both // 2, rows), BF16),
        scratch_shapes=[
            pltpu.VMEM((2, 2, 2, rows, depth), BF16),
            pltpu.VMEM((owners, both, depth), BF16),
            pltpu.SemaphoreType.DMA((2, 2)),
            pltpu.SemaphoreType.DMA((owners,)),
        ],
        compiler_params=pltpu.CompilerParams(vmem_limit_bytes=VMEM_LIMIT),
        name="hidden_units",
    )(place, *a, *b, weights)


def turn_kernel(place_ref, down_ref, out_ref, buf, sems):
    zhi, core = place_ref[0], place_ref[1]
    units = buf.shape[1]
    copies = []
    for k in range(8):
        owner = lax.rem(zhi + 4 - k // 2, 4) * 2 + ((1 - core) if k % 2 else core)
        source = down_ref.at[pl.ds(pl.multiple_of(owner * units, 16), units)]
        copies.append(pltpu.make_async_copy(source, buf.at[k], sems.at[k]))
        copies[-1].start()
    for k in range(0, 8, 4):
        for copy in copies[k : k + 4]:
            copy.wait()
        block = buf[k : k + 4].reshape(4 * units, buf.shape[2])
        out_ref[:, k * units : (k + 4) * units] = block.T


def turned(place, down):
    total, width = down.shape
    return pl.pallas_call(
        turn_kernel,
        in_specs=[pl.BlockSpec(memory_space=pltpu.SMEM), pl.BlockSpec(memory_space=pl.ANY)],
        out_specs=pl.BlockSpec(memory_space=pltpu.VMEM),
        out_shape=jax.ShapeDtypeStruct((width, total), down.dtype),
        scratch_shapes=[pltpu.VMEM((8, total // 8, width), down.dtype), pltpu.SemaphoreType.DMA((8,))],
        compiler_params=pltpu.CompilerParams(vmem_limit_bytes=VMEM_LIMIT),
        name="turned",
    )(place, down)


def down_kernel(*refs):
    h_refs, (down_ref, head_ref, out_ref, buf, sem) = refs[:10], refs[10:]
    units = h_refs[0].shape[0]
    cut = units // 2
    starts = (0, 2 * units, 4 * units, 4 * units + cut, 6 * units)
    for flip in range(2):
        for k, start in enumerate(starts):
            ref = h_refs[flip * 5 + k]
            at = buf.at[pl.ds(start + flip * units, ref.shape[0])]
            pltpu.make_async_copy(ref, at, sem).start()
    pltpu.make_async_copy(buf, buf, sem).wait()
    width = head_ref.shape[0] // 4
    lanes = out_ref.shape[3]
    for side in range(2):
        columns = slice(side * lanes, (side + 1) * lanes)
        product = jnp.dot(down_ref[...], buf[:, columns], preferred_element_type=F32)
        for part in range(4):
            span = slice(part * width, (part + 1) * width)
            out_ref[side, part, :width, :] = product[span, :].astype(BF16)
            along = jnp.sum(product[span, :] * head_ref[span, :], axis=0, keepdims=True)
            high = along.astype(BF16).astype(F32)
            rest = along - high
            middle = rest.astype(BF16).astype(F32)
            low = rest - middle
            pad = jnp.zeros((13, along.shape[1]), F32)
            out_ref[side, part, width:, :] = jnp.concatenate((high, middle, low, pad), axis=0).astype(BF16)


def down_product(pieces, down, head):
    total = pieces[0].shape[1]
    width, depth = down.shape
    anywhere, vmem = pl.BlockSpec(memory_space=pl.ANY), pl.BlockSpec(memory_space=pltpu.VMEM)
    return pl.pallas_call(
        down_kernel,
        in_specs=[anywhere] * 10 + [vmem, vmem],
        out_specs=vmem,
        out_shape=jax.ShapeDtypeStruct((2, 4, width // 4 + 16, total // 2), BF16),
        scratch_shapes=[pltpu.VMEM((depth, total), BF16), pltpu.SemaphoreType.DMA],
        compiler_params=pltpu.CompilerParams(vmem_limit_bytes=VMEM_LIMIT),
        name="down_product",
    )(*pieces, down, head)


def own_kernel(place_ref, *refs):
    a_refs, out_ref, buf, sem = refs[:5], refs[5], refs[6], refs[7]
    y, zlo = place_ref[0], place_ref[1]
    part = a_refs[0].shape[2]

    def fetch(chunk, tile):
        for r in range(4):
            piece = a_refs[2 + tile // 2].at[tile % 2, 0] if r == 2 else a_refs[(0, 1, 0, 4)[r]].at[tile, 0]
            pltpu.make_async_copy(piece, buf.at[pl.ds((chunk * 4 + r) * part, part)], sem).start()

    for chunk in range(2):
        relative = lax.rem(y + 4 - zlo - 2 * chunk + 4, 4)
        for tile in range(4):
            pl.when(relative == tile)(functools.partial(fetch, chunk, tile))
    pltpu.make_async_copy(buf, buf, sem).wait()
    quarter = out_ref.shape[0]
    lanes = pl.ds(pl.multiple_of(y * quarter, 128), quarter)
    out_ref[...] = buf[:, lanes].T.astype(F32)


def own_block(place, a):
    part, depth = a[0].shape[2:]
    anywhere = pl.BlockSpec(memory_space=pl.ANY)
    return pl.pallas_call(
        own_kernel,
        in_specs=[pl.BlockSpec(memory_space=pltpu.SMEM)] + [anywhere] * 5,
        out_specs=pl.BlockSpec(memory_space=pltpu.VMEM),
        out_shape=jax.ShapeDtypeStruct((depth // 4, 8 * part), F32),
        scratch_shapes=[pltpu.VMEM((8 * part, depth), BF16), pltpu.SemaphoreType.DMA],
        name="own_block",
    )(place, *a)


def sums_kernel(arrived_refs, residual_ref, head_ref, out_ref):
    half = residual_ref.shape[0]
    for c, arrived_ref in enumerate(arrived_refs):
        lanes = arrived_ref.shape[2]
        span = slice(c * lanes, (c + 1) * lanes)
        stream = residual_ref[:, span]
        along = jnp.sum(stream * head_ref[...], axis=0, keepdims=True)
        for member in range(arrived_ref.shape[0]):
            stream += arrived_ref[member, :half, :].astype(F32)
            terms = arrived_ref[member, half:, :].astype(F32)
            along += jnp.sum(terms, axis=0, keepdims=True)
        out_ref[0:1, span] = jnp.sum(stream * stream, axis=0, keepdims=True)
        out_ref[1:2, span] = along


def row_sums(arrived, residual, head):
    vmem = pl.BlockSpec(memory_space=pltpu.VMEM)
    return pl.pallas_call(
        sums_kernel,
        in_specs=[[vmem] * len(arrived), vmem, vmem],
        out_specs=vmem,
        out_shape=jax.ShapeDtypeStruct((2, residual.shape[1]), F32),
        name="row_sums",
    )(arrived, residual, head)


def response_weights(flat, segment_ids, section, zlo, y):
    block = segment_ids.shape[0]
    last = jnp.concatenate((flat[1:] != flat[:-1], jnp.ones((1,), bool))).astype(F32)
    sections = [[(model - k) % 4 for k in range(4)] for model in range(4)]

    def ordered(array, library):
        array = array.reshape(4, 2, 2, 2, block).transpose(0, 3, 2, 1, 4)
        parts = [array[at] for around_model in sections for at in around_model]
        return library.stack(parts).reshape(4, 4, 2, 2, 2, block).transpose(0, 2, 3, 1, 4, 5).reshape(1, -1)

    position = jnp.asarray(ordered(np.arange(flat.shape[0], dtype=np.int32), np))
    model = jnp.asarray(np.repeat(np.arange(4, dtype=np.int32), flat.shape[0])[None, :])
    columns, last = ordered(flat, jnp), ordered(last, jnp)
    factor = jnp.where(model == 0, -KL_COEF, jnp.where(model == 1, KL_COEF, jnp.where(model == 2, last, 0.0)))
    own = (((section * 2 + zlo) * 4 + y) * block + jnp.arange(block, dtype=jnp.int32))[:, None]
    reach = (segment_ids[:, None] == columns) & (position >= own)
    to_returns = jnp.where(reach, factor, 0.0)
    to_advantages = jnp.where((model == 3) & (position == own), -1.0, to_returns)
    return to_returns, to_advantages


def shards(rollout_rows, segment_ids, gate_weights, up_weights, down_weights, head_weights):
    section, zhi, core, zlo, y = (lax.axis_index(axis).astype(jnp.int32) for axis in AXES)
    block_rows, width_part = rollout_rows.shape
    owners = 8
    place = jnp.stack((zhi, core, y))

    rows = jnp.stack(around(rollout_rows, "zhi"))
    weights = to_send(gate_weights[0], up_weights[0], owners)
    rows, weights = lax.optimization_barrier((rows, weights))
    other, other_ids = shift(rows, "zlo", 1), shift(segment_ids, "zlo", 1)
    column = jnp.concatenate((jnp.where(zlo == 0, rows, other), jnp.where(zlo == 0, other, rows)), axis=1)
    column, other_ids, weights, down, head = lax.optimization_barrier(
        (column, other_ids, weights, down_weights[0], head_weights[0])
    )
    weights = lax.all_to_all(weights, ("zhi", "core"), split_axis=0, concat_axis=0, tiled=True)

    a = relay(joined(relay(column[:2], "y")), "section")
    b = relay(joined(relay(column[2:], "section")), "y")
    a, b, other_ids = lax.optimization_barrier((a, b, other_ids))

    others = (swapped(a), swapped(b))
    down = turned(place, down)
    head = head.astype(F32)
    quarter = width_part // 4
    own_head = lax.dynamic_slice_in_dim(head, y * quarter, quarter, 0).reshape(quarter, 1)
    head = head.reshape(width_part, 1)
    ids = jnp.stack((jnp.where(zlo == 0, segment_ids, other_ids), jnp.where(zlo == 0, other_ids, segment_ids)))
    ids = jnp.stack(around(jnp.stack(around(ids, "y")), "section"))
    weights, down, head, own_head, ids = lax.optimization_barrier((weights, down, head, own_head, ids))

    places = [jnp.stack((zhi, core, y, jnp.int32(chunk))) for chunk in range(2)]
    x = (a + others[0], b + others[1], weights)
    first = hidden_units(places[0], *x)
    mine = relay(first, "zhi")
    theirs = [shift(first, "core", 1)]
    places[1], theirs[0] = lax.optimization_barrier((places[1], theirs[0]))
    second = hidden_units(places[1], *x)

    own_place, first = lax.optimization_barrier((jnp.stack((y, zlo)), first))
    residual = own_block(own_place, a)
    second, ids = lax.optimization_barrier((second, ids))
    four = jnp.arange(4, dtype=jnp.int32)
    ids = jnp.take(jnp.take(ids, (section - four) % 4, axis=0), (y - four) % 4, axis=1)
    flat = ids.transpose(0, 2, 1, 3).reshape(-1)
    to_returns, to_advantages = response_weights(flat, segment_ids, section, zlo, y)

    cut = second.shape[0] // 2
    one, three = shift(second, "zhi", 1), shift(second, "zhi", 3)
    top, end = one[:cut], three[cut:]
    mine[2], mine[3], _, _ = lax.optimization_barrier((mine[2], mine[3], top, end))
    pieces = [mine + theirs + swapped(mine[1:])]
    mine = [second, one, shift(top, "zhi", 1), shift(end, "zhi", 3), three]
    pieces.append(mine + swapped(mine))
    arrived = []
    for piece in pieces:
        parts = down_product(piece, down, head)
        parts = parts.reshape((8,) + parts.shape[2:])
        if arrived:
            parts, to_returns, to_advantages = lax.optimization_barrier((parts, to_returns, to_advantages))
        arrived.append(lax.all_to_all(parts, ("zlo", "y"), split_axis=0, concat_axis=0, tiled=True))
    lanes = arrived[0].shape[2]
    early = row_sums(arrived[:1], residual[:, :lanes], own_head)
    early = early + shift(early, "core", 1)
    early = total_around(total_around(early, "y"), "zhi")
    late = row_sums(arrived[1:], residual[:, lanes:], own_head)
    late = late + shift(late, "core", 1)
    late = jnp.sum(spread(late, ("zhi", "y")), axis=0)
    sums = jnp.concatenate((early, late), axis=1)
    scores = sums[1] / jnp.sqrt(sums[0] / (width_part * owners) + EPSILON)
    scores = spread(scores, ("section", "zlo")).reshape(1, -1)
    return (jnp.sum(to_advantages * scores, axis=1), jnp.sum(to_returns * scores, axis=1))


def solution(mesh):
    fine = Mesh(mesh.devices.reshape(4, 4, 2, 2, 4), AXES)
    dp, tp, rows = ("zhi", "core"), ("zlo", "y"), ("section", "zlo", "y")
    return jax.shard_map(
        shards,
        mesh=fine,
        in_specs=(
            P(rows, dp),
            P(rows),
            P("section", dp, tp),
            P("section", dp, tp),
            P("section", tp, dp),
            P("section", dp),
        ),
        out_specs=(P(rows), P(rows)),
        check_vma=False,
    )
```
